128 devices in a mesh: ctx: 16 (over y, z), mdl: 8 (over x, core).
Axes of the slice: x: 4, y: 4, z: 4, core: 2. Of those that a mesh axis runs over, the one named last changes fastest.
Arguments:
- queries: bfloat16 [2048, 8192], P('ctx', 'mdl'), may hold values from -6 to 6
- keys: bfloat16 [2048, 8192], P('ctx', 'mdl'), may hold values from -6 to 6
- values: bfloat16 [2048, 8192], P('ctx', 'mdl'), may hold values from -6 to 6
- prefix_state: float32 [64, 128, 128], P('mdl'), may hold values from -64 to 64
- out_gain: bfloat16 [8192], P('mdl'), may hold values from 0.099609375 to 1.8984375
- out_weight: bfloat16 [8192, 6144], P('mdl', 'ctx'), may hold values from -0.0625 to 0.0625
- resid: bfloat16 [2048, 6144], P('ctx', 'mdl'), may hold values from -6 to 6
- ffn_gain: bfloat16 [6144], replicated, may hold values from 0.099609375 to 1.8984375
- expert_ids: int32 [2048, 2], P('ctx'), may hold values from 0 to 7, all different within a row; in each aligned block of 128 rows (0 to 127, 128 to 255, ...) at most 48 rows name the same one
- route_weights: float32 [2048, 2], P('ctx'), may hold values from 0.1 to 1
- gate_weight: bfloat16 [8, 6144, 9216], P('mdl', None, 'ctx'), may hold values from -0.078125 to 0.078125
- up_weight: bfloat16 [8, 6144, 9216], P('mdl', None, 'ctx'), may hold values from -0.078125 to 0.078125
- down_weight: bfloat16 [8, 9216, 6144], P('mdl', 'ctx'), may hold values from -0.0625 to 0.0625
Outputs:
- layer_out: bfloat16 [2048, 6144], P('ctx', 'mdl')
The draws below stay inside these ranges and needn't reach their ends.
Inputs may be any that keep to these rules, and one draw needn't show every extreme that they name: `expert_ids`: each row names 2 different experts. In each aligned block of 128 rows no expert is named by more than 48 rows, a bound that some block reaches.
All inputs are finite; a program needn't handle non-finite values.
Results may differ from the reference program's by a relative error of at most 0.024.
Values may be sent and summed in bfloat16 or wider, within the bound.
No kernel may reach another device: no remote copies, remote signals or barrier semaphores. Data moves between devices by JAX's collectives and lax.ppermute only.
A program may use at most 128 MiB of HBM per device.

```python
import math
import jax
import jax.numpy as jnp
import numpy as np
from jax import lax

D = 6144
HEADS = 64
DH = 128
FF = 9216
TOP = 2
TOK_DEV = 128
TOKENS = 2048
EXPERTS = 8
CAP = 48
FF_DEV = 576
N_CTX = 16


def levels(rng, shape, shards, smallest, high):
    level, own = 1.0, jax.random.fold_in(rng, 6)
    for position, shards_of in shards:
        draws = jnp.exp(jax.random.uniform(jax.random.fold_in(own, position), (shards_of,), jnp.float32, smallest / len(shards), high / len(shards)))
        level = level * jnp.repeat(draws, shape[position] // shards_of).reshape([-1 if axis == position else 1 for axis in range(len(shape))])
    return level


def deal_out(own_key, own, number, rows, number_of, top, most, skew):
    sequence = jax.random.permutation(own_key, number_of)
    packed, ordinary = load_shares(number_of, rows * top, most, skew, True), load_shares(number_of, rows * top, most, skew, False)
    places = jnp.arange(number_of)

    def named(sizes, rotation):
        used = int((sizes > 0).sum())
        fixed = max(1, used // 4)
        passed = fixed + (places - fixed + rotation * (used - fixed)) % max(1, number_of - fixed)
        return jnp.zeros((number_of,), jnp.int32).at[sequence[jnp.where(places < fixed, places, passed)]].set(jnp.asarray(sizes, jnp.int32))

    sizes = jnp.where(number % 4 == 0, named(packed, number // 4), named(ordinary, number - number // 4 - 1))
    mixed = jax.random.permutation(jax.random.fold_in(own, 3), number_of)
    source_of, receiver = mixed[0:number_of // 2 * 2:2], mixed[1:number_of // 2 * 2:2]
    margin = jnp.minimum(sizes[source_of] - 1, most - sizes[receiver]) // 2
    margin = jnp.where((source_of == sequence[0]) | (receiver == sequence[0]) | (sizes[receiver] == 0), 0, jnp.maximum(margin, 0))
    passed = jax.random.randint(jax.random.fold_in(own, 4), (number_of // 2,), 0, 1 << 20) % (margin + 1)
    sizes = sizes.at[source_of].add(-passed).at[receiver].add(passed)
    labels = jnp.searchsorted(jnp.cumsum(sizes), jnp.arange(rows * top), side="right").astype(jnp.int32)
    table = labels.reshape(top, rows).T
    table = table[jax.random.permutation(jax.random.fold_in(own, 1), rows)]
    rotation = jax.random.randint(jax.random.fold_in(own, 2), (rows, 1), 0, top)
    return jnp.take_along_axis(table, (jnp.arange(top)[None, :] + rotation) % top, axis=1)


def load_shares(count, total, bound, slope, full):
    portions = [(1 << 20) // math.isqrt(standing ** slope) + 1 for standing in range(1, count + 1)]
    largest = bound if full else min(bound, max(-(-total // count), total * portions[0] // sum(portions)))
    least = 1 if total - largest >= count - 1 else 0
    holding, rest = [largest] + [least] * (count - 1), total - largest - least * (count - 1)
    while rest > 0:
        candidates = [i for i in range(1, count) if holding[i] < largest] or [i for i in range(1, count) if holding[i] < bound]
        pool, budget = sum([portions[i] for i in candidates]), rest
        for i in candidates:
            more = min(bound - holding[i], max(1, budget * portions[i] // pool), rest)
            holding[i] = holding[i] + more
            rest = rest - more
    return np.array(holding)


def normal_values(key, extent, scale, limit, pieces=(), kind=jnp.bfloat16):
    entries = jax.random.normal(key, extent, jnp.float32) * scale
    if len(pieces) > 0:
        entries = levels(key, extent, pieces, -0.22, 0.18) * entries
    return jnp.clip(entries, min=-limit, max=limit).astype(kind)


def setup_inputs(seed: int = 0) -> dict:
    key_of = jax.random.split(jax.random.key(seed), 14)
    queries = normal_values(key_of[0], (TOKENS, HEADS * DH), 1.0, 6.0, ((0, 16), (1, 8)))
    keys = normal_values(key_of[1], (TOKENS, HEADS * DH), 1.0, 6.0, ((0, 16), (1, 8)))
    values = normal_values(key_of[2], (TOKENS, HEADS * DH), 1.0, 6.0, ((0, 16), (1, 8)))
    prefix_state = normal_values(key_of[3], (HEADS, DH, DH), 12.0, 64.0, ((0, 8),), jnp.float32)
    out_gain = jnp.clip(1.0 + 0.18 * jax.random.normal(key_of[4], (HEADS * DH,), jnp.float32), 0.099609375, 1.8984375).astype(jnp.bfloat16)
    out_weight = normal_values(key_of[5], (HEADS * DH, D), (HEADS * DH) ** -0.5, 0.0625, ((0, 8), (1, 16)))
    resid = normal_values(key_of[6], (TOKENS, D), 1.0, 6.0, ((0, 16), (1, 8)))
    ffn_gain = jnp.clip(1.0 + 0.18 * jax.random.normal(key_of[7], (D,), jnp.float32), 0.099609375, 1.8984375).astype(jnp.bfloat16)
    expert_ids_keys = jax.random.split(jax.random.fold_in(key_of[8], 1), TOKENS // TOK_DEV)
    expert_ids_turns = jax.random.permutation(jax.random.fold_in(key_of[8], 3), TOKENS // TOK_DEV)
    expert_ids = jax.vmap(lambda own, number: deal_out(jax.random.fold_in(key_of[8], 2), own, number, TOK_DEV, EXPERTS, TOP, CAP, 2))(expert_ids_keys, expert_ids_turns).reshape((TOKENS, TOP))
    route_weights = jnp.clip(jnp.exp(math.log(1.0) - 2.3025851 * jax.random.uniform(key_of[9], (TOKENS, TOP), jnp.float32) ** levels(key_of[9], (TOKENS, TOP), ((0, 16),), -0.2, 0.2)), 0.1, 1.0)
    gate_weight = normal_values(key_of[10], (EXPERTS, D, FF), D ** -0.5, 0.078125, ((0, 8), (2, 16)))
    up_weight = normal_values(key_of[11], (EXPERTS, D, FF), D ** -0.5, 0.078125, ((0, 8), (2, 16)))
    down_weight = normal_values(key_of[12], (EXPERTS, FF, D), FF ** -0.5, 0.0625, ((0, 8), (1, 16)))
    return dict(queries=queries, keys=keys, values=values, prefix_state=prefix_state, out_gain=out_gain, out_weight=out_weight, resid=resid, ffn_gain=ffn_gain, expert_ids=expert_ids, route_weights=route_weights, gate_weight=gate_weight, up_weight=up_weight, down_weight=down_weight)


epsilon = 1e-06
highest = lax.Precision.HIGHEST

def to_bf16_and_back(array):
    rounded = lax.optimization_barrier(array.astype(jnp.bfloat16))
    return rounded.astype(jnp.float32)

def reference(queries, keys, values, prefix_state, out_gain, out_weight, resid, ffn_gain, expert_ids, route_weights, gate_weight, up_weight, down_weight):
    q_blocks = queries.astype(jnp.float32).reshape(N_CTX, TOK_DEV, HEADS, DH)
    k_blocks = keys.astype(jnp.float32).reshape(N_CTX, TOK_DEV, HEADS, DH)
    v_blocks = values.astype(jnp.float32).reshape(N_CTX, TOK_DEV, HEADS, DH)
    span_state = jnp.einsum('bthd,bthe->bhde', k_blocks, v_blocks, precision=highest)
    running = jnp.cumsum(span_state, axis=0)
    earlier = jnp.concatenate([jnp.zeros_like(span_state[:1]), running[:-1]], axis=0)
    carried = to_bf16_and_back(prefix_state[None] + earlier)
    scores = jnp.einsum('bthd,bshd->bhts', q_blocks, k_blocks, precision=highest)
    causal = jnp.arange(TOK_DEV)[:, None] >= jnp.arange(TOK_DEV)[None, :]
    scores = to_bf16_and_back(jnp.where(causal[None, None], scores, 0.0))
    intra = jnp.einsum('bhts,bshd->bthd', scores, v_blocks, precision=highest)
    inter = jnp.einsum('bthd,bhde->bthe', q_blocks, carried, precision=highest)
    raw = intra + inter
    norm_scale = lax.rsqrt(lax.optimization_barrier(jnp.mean(raw * raw, axis=3, keepdims=True)) + epsilon)
    attn = raw * norm_scale * out_gain.astype(jnp.float32).reshape(HEADS, DH)
    attn = attn.astype(jnp.bfloat16).reshape(TOKENS, HEADS * DH)
    projected = jnp.dot(attn, out_weight, preferred_element_type=jnp.float32)
    hidden_one = (resid.astype(jnp.float32) + projected).astype(jnp.bfloat16)
    hidden_float = hidden_one.astype(jnp.float32)
    normed = hidden_float * lax.rsqrt(lax.optimization_barrier(jnp.mean(hidden_float * hidden_float, axis=1, keepdims=True)) + epsilon)
    normed = (normed * ffn_gain.astype(jnp.float32)).astype(jnp.bfloat16)
    normed_blocks = normed.astype(jnp.float32).reshape(N_CTX, TOK_DEV, D)
    id_blocks = expert_ids.reshape(N_CTX, TOK_DEV, TOP)
    weight_blocks = route_weights.reshape(N_CTX, TOK_DEV, TOP)
    chosen = id_blocks[:, :, :, None] == jnp.arange(EXPERTS, dtype=jnp.int32)[None, None, None, :]
    uses_count = lax.optimization_barrier(jnp.sum(chosen.astype(jnp.int32), axis=2))
    slot_index = (jnp.cumsum(uses_count, axis=1) - uses_count).astype(jnp.int32)
    weight_by_expert = lax.optimization_barrier(jnp.sum(jnp.where(chosen, weight_blocks[:, :, :, None], jnp.float32(0.0)), axis=2))
    slot_range = jnp.arange(CAP, dtype=jnp.int32)
    mixture = jnp.zeros((N_CTX, TOK_DEV, D), jnp.float32)
    for expert in range(EXPERTS):
        placing = (uses_count[:, None, :, expert] == 1) & (slot_index[:, None, :, expert] == slot_range[None, :, None])
        placing = placing.astype(jnp.float32)
        dispatched = jnp.einsum('bst,btd->bsd', placing, normed_blocks, precision=highest)
        dispatched = dispatched.astype(jnp.bfloat16).reshape(N_CTX * CAP, D)
        gate_part = jnp.dot(dispatched, gate_weight[expert], preferred_element_type=jnp.float32)
        up_part = jnp.dot(dispatched, up_weight[expert], preferred_element_type=jnp.float32)
        inner = (jax.nn.silu(gate_part) * up_part).astype(jnp.bfloat16)
        grouped = jnp.einsum('rgf,gfd->rgd', inner.astype(jnp.float32).reshape(N_CTX * CAP, N_CTX, FF_DEV), down_weight[expert].astype(jnp.float32).reshape(N_CTX, FF_DEV, D), precision=highest)
        expert_out = lax.optimization_barrier(jnp.sum(to_bf16_and_back(grouped), axis=1)).reshape(N_CTX, CAP, D)
        spread = placing * weight_by_expert[:, None, :, expert]
        mixture = mixture + jnp.einsum('bst,bsd->btd', spread, expert_out, precision=highest)
    return (hidden_float + mixture.reshape(TOKENS, D)).astype(jnp.bfloat16)
```

```python
import jax
import jax.numpy as jnp
from jax import lax
from jax.sharding import PartitionSpec as P

DH = 128
TOP = 2
N = 4

epsilon = 1e-06
f32 = jnp.float32
bf16 = jnp.bfloat16


def move_z(v, s):
    return lax.ppermute(v, "ctx", [(y * N + z, y * N + (z + s) % N) for y in range(N) for z in range(N)])


def move_y(v, s):
    return lax.ppermute(v, "ctx", [(y * N + z, (y + s) % N * N + z) for y in range(N) for z in range(N)])


def move_m(v, s, flip):
    return lax.ppermute(v, "mdl", [(x * 2 + c, (x + s) % N * 2 + (c ^ flip)) for x in range(N) for c in range(2)])


def swap_xy(v):
    pairs = []
    for y in range(N):
        for z in range(N):
            for x in range(N):
                for c in range(2):
                    pairs.append(((y * N + z) * 8 + x * 2 + c, (x * N + z) * 8 + y * 2 + c))
    return lax.ppermute(v, ("ctx", "mdl"), pairs)


def in_order(parts, at, axis):
    turned = [parts[3], parts[2], parts[1], parts[0]]
    size = parts[0].shape[axis]
    both = jnp.concatenate(turned + turned[:3], axis=axis)
    return lax.dynamic_slice_in_dim(both, (3 - at) * size, 4 * size, axis=axis)


def ring_gather(v, move):
    half = v.shape[0] // 2
    back, ahead = move(v, 1), move(v, -1)
    far = jnp.concatenate([move(back[:half], 1), move(ahead[half:], -1)], axis=0)
    return [v, back, far, ahead]


def ring_scatter(parts, move):
    half = parts[2].shape[0] // 2
    wide = parts[2].astype(bf16)
    a = move(wide[:half], 1)
    b = move(wide[half:], -1)
    p1, p3 = parts[1].astype(f32), parts[3].astype(f32)
    ahead = jnp.concatenate([p1[:half] + a.astype(f32), p1[half:]], axis=0).astype(bf16)
    behind = jnp.concatenate([p3[:half], p3[half:] + b.astype(f32)], axis=0).astype(bf16)
    return parts[0].astype(f32) + move(ahead, 1).astype(f32) + move(behind, -1).astype(f32)


def carried_state(span, prefix_state, y, z):
    quarter = span.shape[0] // N
    span = span.astype(bf16)

    def cut(a, q):
        return lax.dynamic_slice_in_dim(a, q % N * quarter, quarter, axis=0)

    mine = [cut(span, z).astype(f32)]
    for s in (1, 2, 3):
        mine.append(move_z(cut(span, z + s), s).astype(f32))
    total = (mine[0] + mine[1] + mine[2] + mine[3]).astype(bf16)
    base = cut(prefix_state, z)
    for s in (1, 2, 3):
        base = base + jnp.where((y - s) % N < y, move_y(total, s).astype(f32), 0.0)
    out = []
    for r in range(N):
        target = (z + r) % N
        acc = base
        for s in range(N):
            acc = acc + jnp.where((z - s) % N < target, mine[s], 0.0)
        acc = acc.astype(bf16)
        out.append(acc if r == 0 else move_z(acc, r))
    return in_order(out, z, 0)


def attention(queries, keys, values, prefix_state, out_gain, y, z):
    rows = queries.shape[0]
    heads = queries.shape[1] // DH
    q = queries.reshape(rows, heads, DH)
    k = keys.reshape(rows, heads, DH)
    v = values.reshape(rows, heads, DH)
    span = jnp.einsum("thd,the->hde", k, v, preferred_element_type=f32)
    carried = carried_state(span, prefix_state, y, z)
    scores = jnp.einsum("thd,shd->hts", q, k, preferred_element_type=f32)
    causal = jnp.arange(rows)[:, None] >= jnp.arange(rows)[None, :]
    scores = jnp.where(causal[None], scores, 0.0).astype(bf16)
    intra = jnp.einsum("hts,shd->thd", scores, v, preferred_element_type=f32)
    inter = jnp.einsum("thd,hde->the", q, carried, preferred_element_type=f32)
    raw = intra + inter
    scale = lax.rsqrt(jnp.mean(raw * raw, axis=2, keepdims=True) + epsilon)
    attn = raw * scale * out_gain.astype(f32).reshape(heads, DH)
    return attn.astype(bf16).reshape(rows, heads * DH)


def per_device(
    queries,
    keys,
    values,
    prefix_state,
    out_gain,
    out_weight,
    resid,
    ffn_gain,
    expert_ids,
    route_weights,
    gate_weight,
    up_weight,
    down_weight,
):
    ctx, mdl = lax.axis_index("ctx"), lax.axis_index("mdl")
    y, z = ctx // N, ctx % N
    x, c = mdl // 2, mdl % 2
    rows = queries.shape[0]
    cols = resid.shape[1]
    experts = 2 * N
    cap = 3 * rows * TOP // (2 * experts)
    places = [(s, flip) for s in range(N) for flip in range(2)]

    own_resid = swap_xy(resid)
    routing = jnp.concatenate([expert_ids.astype(f32), route_weights], axis=1)
    routing = lax.all_gather(routing, "ctx")[x * N + z]
    ids, weights = routing[:, :TOP].astype(jnp.int32), routing[:, TOP:]
    chosen = ids[:, :, None] == jnp.arange(experts, dtype=jnp.int32)
    uses = jnp.sum(chosen.astype(jnp.int32), axis=1)
    slots = jnp.cumsum(uses, axis=0) - uses
    slot_of = jnp.sum(jnp.where(chosen, slots[:, None, :], 0), axis=2)

    w_parts = ring_gather(out_weight, move_z)
    w_full = in_order(w_parts, z, 1)
    attn = attention(queries, keys, values, prefix_state, out_gain, y, z)
    a_full = in_order(ring_gather(attn, move_y), y, 0)
    partial = jnp.dot(a_full, w_full, preferred_element_type=f32).astype(bf16)
    partial = partial.reshape(N, rows, 2, cols)
    kept = lax.dynamic_index_in_dim(partial, c, axis=2, keepdims=False)
    given = lax.dynamic_index_in_dim(partial, 1 - c, axis=2, keepdims=False)
    pair = (kept.astype(f32) + move_m(given, 0, 1).astype(f32)).astype(bf16)
    summed = own_resid.astype(f32) + lax.dynamic_index_in_dim(pair, x, 0, keepdims=False).astype(f32)
    for s in (1, 2, 3):
        piece = lax.dynamic_index_in_dim(pair, (x + s) % N, 0, keepdims=False)
        summed = summed + move_m(piece, s, 0).astype(f32)
    hidden_one = summed.astype(bf16)

    slot_range = jnp.arange(cap, dtype=jnp.int32)
    dispatched = [[None, None] for _ in range(N)]
    for s, flip in places:
        expert = (x + s) % N * 2 + (c ^ flip)
        placing = jnp.any((ids[None] == expert) & (slot_of[None] == slot_range[:, None, None]), axis=2)
        picked = jnp.dot(placing.astype(bf16), hidden_one, preferred_element_type=f32).astype(bf16)
        dispatched[s][flip] = picked if (s, flip) == (0, 0) else move_m(picked, s, flip)
    tiles = []
    gain = lax.dynamic_slice_in_dim(ffn_gain, y * 2 * cols, 2 * cols, 0).astype(f32)
    squares = []
    for s in range(N):
        same, other = dispatched[s]
        tile = jnp.concatenate([jnp.where(c == 0, same, other), jnp.where(c == 0, other, same)], axis=1).astype(f32)
        squares.append(jnp.sum(tile * tile, axis=1))
        tiles.append((tile * gain).astype(bf16))
    squares = lax.all_gather(jnp.stack(squares), "ctx").reshape(N, N, N, cap)
    squares = jnp.sum(squares, axis=0)
    row_scale = lax.rsqrt(squares / (2 * N * cols) + epsilon)

    w_gate, w_up, w_down = gate_weight[0], up_weight[0], down_weight[0]

    def gather(first, second):
        over_z = ring_gather(first, move_z)
        over_y = ring_gather(second, move_y)
        one = ring_gather(jnp.concatenate(over_z, axis=0), move_y)
        two = ring_gather(jnp.concatenate([over_y[k] for k in range(N)], axis=0), move_z)
        full = []
        for k in range(N):
            here = [one[k]]
            for j in range(N):
                here.append(two[j][k * cap : (k + 1) * cap])
            full.append(jnp.concatenate(here, axis=0))
        return in_order(full, y, 1)

    def scale_rows(i):
        order = [lax.dynamic_index_in_dim(row_scale, (z - k) % N, 0, keepdims=False)[i] for k in range(N)]
        return jnp.concatenate(order)

    def experts_on(xs, i):
        scale = jnp.concatenate([scale_rows(i), scale_rows(i + 1)])[:, None]
        gate = jnp.dot(xs, w_gate, preferred_element_type=f32) * scale
        up = jnp.dot(xs, w_up, preferred_element_type=f32) * scale
        inner = (jax.nn.silu(gate) * up).astype(bf16)
        return jnp.dot(inner, w_down, preferred_element_type=f32).astype(bf16)

    def scatter(out):
        one, two = out[: N * cap], out[N * cap :]
        width = 2 * cols
        by_y = [lax.dynamic_slice_in_dim(one, (y + r) % N * width, width, axis=1) for r in range(N)]
        one = ring_scatter(by_y, move_y)
        one = one.reshape(N, cap, width)
        one = ring_scatter([one[(N - r) % N] for r in range(N)], move_z)
        two = two.reshape(N, cap, N * width)
        two = ring_scatter([two[(N - r) % N] for r in range(N)], move_z)
        by_y = [lax.dynamic_slice_in_dim(two, (y + r) % N * width, width, axis=1) for r in range(N)]
        two = ring_scatter(by_y, move_y)
        return one, two

    xs = [gather(tiles[i], tiles[i + 1]) for i in (0, 2)]
    outs = [experts_on(xs[i // 2], i) for i in (0, 2)]
    back = []
    for o in outs:
        back += scatter(o)

    mixture = 0.0
    for s, flip in places:
        piece = back[(N - s) % N].astype(bf16)
        piece = lax.dynamic_slice_in_dim(piece, (c ^ flip) * cols, cols, axis=1)
        piece = piece if (s, flip) == (0, 0) else move_m(piece, s, flip)
        expert = (x - s) % N * 2 + (c ^ flip)
        for j in range(TOP):
            taken = (ids[:, j : j + 1] == expert) & (slot_of[:, j : j + 1] == slot_range[None, :])
            mixture = mixture + weights[:, j : j + 1] * jnp.dot(taken.astype(bf16), piece, preferred_element_type=f32)
    layer_out = (hidden_one.astype(f32) + mixture).astype(bf16)
    return swap_xy(layer_out)


def solution(mesh):
    placed = (
        P("ctx", "mdl"),
        P("ctx", "mdl"),
        P("ctx", "mdl"),
        P("mdl", None, None),
        P("mdl"),
        P("mdl", "ctx"),
        P("ctx", "mdl"),
        P(),
        P("ctx", None),
        P("ctx", None),
        P("mdl", None, "ctx"),
        P("mdl", None, "ctx"),
        P("mdl", "ctx", None),
    )
    return jax.shard_map(
        per_device, mesh=mesh, in_specs=placed, out_specs=P("ctx", "mdl"), check_vma=False
    )
```

```python
import jax
import jax.numpy as jnp
from jax import lax
from jax.experimental import pallas as pl
from jax.experimental.pallas import tpu as pltpu
from jax.sharding import PartitionSpec as P

DH = 128
TOP = 2
N = 4

VMEM = 56 * 1024 * 1024

epsilon = 1e-06
f32 = jnp.float32
bf16 = jnp.bfloat16


def move_z(v, s):
    return lax.ppermute(v, "ctx", [(y * N + z, y * N + (z + s) % N) for y in range(N) for z in range(N)])


def move_y(v, s):
    return lax.ppermute(v, "ctx", [(y * N + z, (y + s) % N * N + z) for y in range(N) for z in range(N)])


def move_m(v, s, flip):
    return lax.ppermute(v, "mdl", [(x * 2 + c, (x + s) % N * 2 + (c ^ flip)) for x in range(N) for c in range(2)])


def swap_xy(v):
    pairs = []
    for y in range(N):
        for z in range(N):
            for x in range(N):
                for c in range(2):
                    pairs.append(((y * N + z) * 8 + x * 2 + c, (x * N + z) * 8 + y * 2 + c))
    return lax.ppermute(v, ("ctx", "mdl"), pairs)


def carried_state(span, prefix_state, y, z):
    quarter = span.shape[0] // N
    span = span.astype(bf16)

    def cut(a, q):
        return lax.dynamic_slice_in_dim(a, q % N * quarter, quarter, axis=0)

    mine = [cut(span, z).astype(f32)]
    for s in (1, 2, 3):
        mine.append(move_z(cut(span, z + s), s).astype(f32))
    total = (mine[0] + mine[1] + mine[2] + mine[3]).astype(bf16)
    base = cut(prefix_state, z)
    for s in (1, 2, 3):
        base = base + jnp.where((y - s) % N < y, move_y(total, s).astype(f32), 0.0)
    out = []
    for r in range(N):
        target = (z + r) % N
        acc = base
        for s in range(N):
            acc = acc + jnp.where((z - s) % N < target, mine[s], 0.0)
        acc = acc.astype(bf16)
        out.append(acc if r == 0 else move_z(acc, r))
    turned = jnp.concatenate([out[3], out[2], out[1], out[0], out[3], out[2], out[1]], axis=0)
    return lax.dynamic_slice_in_dim(turned, (3 - z) * quarter, N * quarter, axis=0)


def attention(queries, keys, values, prefix_state, out_gain, y, z):
    rows = queries.shape[0]
    heads = queries.shape[1] // DH
    q = queries.reshape(rows, heads, DH)
    k = keys.reshape(rows, heads, DH)
    v = values.reshape(rows, heads, DH)
    span = jnp.einsum("thd,the->hde", k, v, preferred_element_type=f32)
    carried = carried_state(span, prefix_state, y, z)
    scores = jnp.einsum("thd,shd->hts", q, k, preferred_element_type=f32)
    causal = jnp.arange(rows)[:, None] >= jnp.arange(rows)[None, :]
    scores = jnp.where(causal[None], scores, 0.0).astype(bf16)
    intra = jnp.einsum("hts,shd->thd", scores, v, preferred_element_type=f32)
    inter = jnp.einsum("thd,hde->the", q, carried, preferred_element_type=f32)
    raw = intra + inter
    scale = lax.rsqrt(jnp.mean(raw * raw, axis=2, keepdims=True) + epsilon)
    attn = raw * scale * out_gain.astype(f32).reshape(heads, DH)
    return attn.astype(bf16).reshape(rows, heads * DH)


def full(shape):
    return pl.BlockSpec(shape, lambda g, *_: (0,) * len(shape))


def project(blocks, w_full, y, c):
    rows, depth = blocks[0].shape
    cols = w_full.shape[1] // 2

    def kernel(at, *refs):
        w, out = refs[N], refs[N + 1]
        x = jnp.concatenate([refs[k][...] for k in range(N)], axis=0)
        res = jnp.dot(x, w[...], preferred_element_type=f32).astype(bf16)
        for k in range(N):
            out[0, pl.ds(pl.multiple_of(at[2 + k] * rows, rows), rows), :] = res[k * rows : (k + 1) * rows]

    at = jnp.stack([1 - c, c] + [(y - k) % N for k in range(N)]).astype(jnp.int32)
    return pl.pallas_call(
        kernel,
        grid_spec=pltpu.PrefetchScalarGridSpec(
            num_scalar_prefetch=1,
            grid=(2,),
            in_specs=[full((rows, depth))] * N + [pl.BlockSpec((depth, cols), lambda g, at: (0, at[g]))],
            out_specs=pl.BlockSpec((1, N * rows, cols), lambda g, at: (g, 0, 0)),
        ),
        out_shape=jax.ShapeDtypeStruct((2, N * rows, cols), bf16),
        compiler_params=pltpu.CompilerParams(vmem_limit_bytes=VMEM),
        name="project",
    )(at, *blocks, w_full)


def gate_up(y, sums, first, second, w_gate, w_up, gain, last):
    width, hidden = w_gate.shape[0] // (2 * N), w_gate.shape[1]
    rows = first[0][1][0].shape[0] * len(first[0][1])
    quarter = rows // N
    chunks = [p for _, parts in first + second for p in parts]
    n_first = len(first)
    steps = n_first + N
    n_sums = 0 if sums is None else 3

    def kernel(at, *refs):
        refs = list(refs)
        held = [refs.pop(0) for _ in range(n_sums)]
        own = [refs.pop(0) for _ in chunks]
        wg, wu, gn = refs[0], refs[1], refs[2]
        if last:
            inner, a_gate, a_up, a_sq = refs[3:]
        else:
            a_gate, a_up, a_sq = refs[3:]
        g = pl.program_id(0)

        @pl.when(g == 0)
        def _():
            if n_sums:
                a_gate[...] = held[0][...]
                a_up[...] = held[1][...]
                a_sq[...] = held[2][...]
            else:
                a_gate[...] = jnp.zeros_like(a_gate)
                a_up[...] = jnp.zeros_like(a_up)
                a_sq[...] = jnp.zeros_like(a_sq)

        def add(x, places):
            x = x.astype(f32)
            sq = jnp.sum(x * x, axis=1, keepdims=True)
            xg = (x * gn[0].astype(f32)).astype(bf16)
            dg = jnp.dot(xg, wg[...], preferred_element_type=f32)
            du = jnp.dot(xg, wu[...], preferred_element_type=f32)
            at_row = 0
            for start, size in places:
                to = pl.ds(start, size)
                a_gate[to, :] += dg[at_row : at_row + size]
                a_up[to, :] += du[at_row : at_row + size]
                a_sq[to, :] += jnp.broadcast_to(sq[at_row : at_row + size], (size, 128))
                at_row += size

        taken = 0
        for n, (_, parts) in enumerate(first):
            mine = own[taken : taken + len(parts)]
            taken += len(parts)

            @pl.when(g == n)
            def _(mine=mine):
                add(jnp.concatenate([r[...] for r in mine], axis=0), [(0, rows)])

        rest = []
        for k, parts in second:
            rest.append((k, own[taken : taken + len(parts)]))
            taken += len(parts)
        for j in range(N):

            @pl.when(g == n_first + j)
            def _(j=j):
                xs, places = [], []
                for k, mine in rest:
                    per = N // len(mine)
                    xs.append(mine[j // per][j % per * quarter : (j % per + 1) * quarter, :])
                    places.append((k * quarter, quarter))
                add(jnp.concatenate(xs, axis=0), places)

        if last:

            @pl.when(g == steps - 1)
            def _():
                scale = lax.rsqrt(a_sq[:, :1] / (2 * N * width) + epsilon)
                gate = a_gate[...] * scale
                up = a_up[...] * scale
                inner[...] = (gate / (1.0 + jnp.exp(-gate)) * up).astype(bf16)

    at = jnp.stack([2 * ((y - k) % N) for k, _ in first] + [2 * ((y - j) % N) + 1 for j in range(N)])
    acc = (rows, hidden)
    sq = (rows, 128)
    w_spec = pl.BlockSpec((width, hidden), lambda g, at: (at[g], 0))
    out_shape = [jax.ShapeDtypeStruct(acc, f32), jax.ShapeDtypeStruct(acc, f32), jax.ShapeDtypeStruct(sq, f32)]
    out_specs = [full(acc), full(acc), full(sq)]
    scratch = []
    if last:
        out_shape, out_specs = [jax.ShapeDtypeStruct(acc, bf16)], [full(acc)]
        scratch = [pltpu.VMEM(acc, f32), pltpu.VMEM(acc, f32), pltpu.VMEM(sq, f32)]
    res = pl.pallas_call(
        kernel,
        grid_spec=pltpu.PrefetchScalarGridSpec(
            num_scalar_prefetch=1,
            grid=(steps,),
            in_specs=([full(acc), full(acc), full(sq)] if n_sums else [])
            + [full(p.shape) for p in chunks]
            + [w_spec, w_spec, pl.BlockSpec((1, 1, width), lambda g, at: (at[g], 0, 0))],
            out_specs=out_specs,
            scratch_shapes=scratch,
        ),
        out_shape=out_shape,
        compiler_params=pltpu.CompilerParams(vmem_limit_bytes=VMEM),
        name="gate_up",
    )(at.astype(jnp.int32), *(sums or ()), *chunks, w_gate, w_up, gain.reshape(2 * N, 1, width))
    return res[0] if last else tuple(res)


def down(y, inner, w_down, ahead, halves):
    rows, hidden = inner.shape
    quarter = rows // N
    width = w_down.shape[1] // (2 * N)
    n = len(ahead)

    def kernel(at, x, w, *outs):
        g = pl.program_id(0)
        per = 2 if halves else 1

        def put(which, start, res):
            size = rows // per
            for p in range(per):
                low, high = max(start, p * size), min(start + res.shape[0], (p + 1) * size)
                if low < high:
                    outs[which * per + p][low - p * size : high - p * size, :] = res[low - start : high - start]

        for i in range(n):

            @pl.when(g == i)
            def _(i=i):
                put(i, 0, jnp.dot(x[...], w[...], preferred_element_type=f32).astype(bf16))

        for j in range(N):

            @pl.when(g == n + j)
            def _(j=j):
                starts = [(N - r) % N * quarter for r in ahead]
                xs = jnp.concatenate([x[s : s + quarter, :] for s in starts], axis=0)
                res = jnp.dot(xs, w[...], preferred_element_type=f32).astype(bf16)
                for i in range(n):
                    put(n + i, j * quarter, res[i * quarter : (i + 1) * quarter])

    at = jnp.stack([2 * ((y + r) % N) for r in ahead] + [2 * ((y + j) % N) + 1 for j in range(N)])
    per = 2 if halves else 1
    shape = (rows // per, width)
    return pl.pallas_call(
        kernel,
        grid_spec=pltpu.PrefetchScalarGridSpec(
            num_scalar_prefetch=1,
            grid=(n + N,),
            in_specs=[full((rows, hidden)), pl.BlockSpec((hidden, width), lambda g, at: (0, at[g]))],
            out_specs=[full(shape)] * (2 * n * per),
        ),
        out_shape=[jax.ShapeDtypeStruct(shape, bf16)] * (2 * n * per),
        compiler_params=pltpu.CompilerParams(vmem_limit_bytes=VMEM),
        name="down",
    )(at.astype(jnp.int32), inner, w_down)


def merge(ahead, behind, a, b):
    half, width = a.shape

    def kernel(p, q, a_ref, b_ref, p_out, q_out):
        g = pl.program_id(0)

        @pl.when(g == 0)
        def _():
            p_out[...] = (p[...].astype(f32) + a_ref[...].astype(f32)).astype(bf16)
            q_out[...] = q[...]

        @pl.when(g == 1)
        def _():
            p_out[...] = p[...]
            q_out[...] = (q[...].astype(f32) + b_ref[...].astype(f32)).astype(bf16)

    block = pl.BlockSpec((half, width), lambda g: (g, 0))
    return pl.pallas_call(
        kernel,
        grid=(2,),
        in_specs=[block, block, full(a.shape), full(a.shape)],
        out_specs=[block, block],
        out_shape=[jax.ShapeDtypeStruct(ahead.shape, bf16)] * 2,
        compiler_params=pltpu.CompilerParams(vmem_limit_bytes=VMEM),
        name="merge",
    )(ahead, behind, a, b)


def sum_parts(own, a, b):
    return (own.astype(f32) + a.astype(f32) + b.astype(f32)).astype(bf16)


def experts_out(one, two, y, w_gate, w_up, w_down, gain):
    half = one.shape[0] // 2
    one1, one3 = move_z(one, 1), move_z(one, -1)
    two1, two3 = move_y(two, 1), move_y(two, -1)
    one2a, one2b = move_z(one1[:half], 1), move_z(one3[half:], -1)
    two2a, two2b = move_y(two1[:half], 1), move_y(two3[half:], -1)
    a0 = jnp.concatenate([one, one1, one2a, one2b, one3], axis=0)
    b0 = jnp.concatenate([two, two1, two2a, two2b, two3], axis=0)
    half = a0.shape[0] // 2
    a1, a3 = move_y(a0, 1), move_y(a0, -1)
    b1, b3 = move_z(b0, 1), move_z(b0, -1)
    sums = gate_up(y, None, [(0, [a0])], [(0, [b0])], w_gate, w_up, gain, False)
    a2 = [move_y(a1[:half], 1), move_y(a3[half:], -1)]
    b2 = [move_z(b1[:half], 1), move_z(b3[half:], -1)]
    sums = gate_up(y, sums, [(1, [a1]), (3, [a3])], [(1, [b1]), (3, [b3])], w_gate, w_up, gain, False)
    inner = gate_up(y, sums, [(2, a2)], [(2, b2)], w_gate, w_up, gain, True)
    p2a, p2b, q2a, q2b = down(y, inner, w_down, [2], True)
    p2a, p2b = move_y(p2a, 1), move_y(p2b, -1)
    q2a, q2b = move_z(q2a, 1), move_z(q2b, -1)
    p1, p3, q1, q3 = down(y, inner, w_down, [1, 3], False)
    p1, p3 = merge(p1, p3, p2a, p2b)
    q1, q3 = merge(q1, q3, q2a, q2b)
    p1, p3 = move_y(p1, 1), move_y(p3, -1)
    q1, q3 = move_z(q1, 1), move_z(q3, -1)
    p0, q0 = down(y, inner, w_down, [0], False)
    p = sum_parts(p0, p1, p3).reshape(N, -1, p0.shape[1])
    q = sum_parts(q0, q1, q3).reshape(N, -1, q0.shape[1])
    half = p.shape[1] // 2
    p2a, p2b = move_z(p[2][:half], 1), move_z(p[2][half:], -1)
    q2a, q2b = move_y(q[2][:half], 1), move_y(q[2][half:], -1)
    p1, p3 = merge(p[3], p[1], p2a, p2b)
    q1, q3 = merge(q[1], q[3], q2a, q2b)
    p1, p3 = move_z(p1, 1), move_z(p3, -1)
    q1, q3 = move_y(q1, 1), move_y(q3, -1)
    return sum_parts(p[0], p1, p3), sum_parts(q[0], q1, q3)


def per_device(
    queries,
    keys,
    values,
    prefix_state,
    out_gain,
    out_weight,
    resid,
    ffn_gain,
    expert_ids,
    route_weights,
    gate_weight,
    up_weight,
    down_weight,
):
    ctx, mdl = lax.axis_index("ctx"), lax.axis_index("mdl")
    y, z = ctx // N, ctx % N
    x, c = mdl // 2, mdl % 2
    rows = queries.shape[0]
    cols = resid.shape[1]
    experts = 2 * N
    cap = 3 * rows * TOP // (2 * experts)

    groups_z = [[a * N + b for b in range(N)] for a in range(N)]
    groups_x = [[a * 2 + b for a in range(N)] for b in range(2)]
    w_full = lax.all_gather(out_weight, "ctx", axis=1, tiled=True, axis_index_groups=groups_z)
    attn = attention(queries, keys, values, prefix_state, out_gain, y, z)

    own_resid = swap_xy(resid)
    routing = swap_xy(jnp.concatenate([expert_ids.astype(f32), route_weights], axis=1))
    ids, weights = routing[:, :TOP].astype(jnp.int32), routing[:, TOP:]
    chosen = ids[:, :, None] == jnp.arange(experts, dtype=jnp.int32)
    uses = jnp.sum(chosen.astype(jnp.int32), axis=1)
    slots = jnp.cumsum(uses, axis=0) - uses
    slot_of = jnp.sum(jnp.where(chosen, slots[:, None, :], 0), axis=2)
    place = ids * cap + slot_of
    taken = place[:, :, None] == jnp.arange(experts * cap, dtype=jnp.int32)
    placing = jnp.any(taken, axis=1).astype(bf16).T

    blocks = [attn] + [move_y(attn, s) for s in (1, 2, 3)]
    given, kept = project(blocks, w_full, y, c)
    pair = (kept.astype(f32) + move_m(given, 0, 1).astype(f32)).astype(bf16)
    pair = lax.all_to_all(pair, "mdl", 0, 0, tiled=True, axis_index_groups=groups_x)
    summed = jnp.sum(pair.reshape(N, rows, cols).astype(f32), axis=0)
    hidden_one = (own_resid.astype(f32) + summed).astype(bf16)

    picked = jnp.dot(placing, hidden_one, preferred_element_type=f32).astype(bf16)
    picked = lax.all_to_all(picked, "mdl", 0, 0, tiled=True).reshape(N, 2, cap, cols)
    one, two = picked[:, 0].reshape(N * cap, cols), picked[:, 1].reshape(N * cap, cols)
    one, two = experts_out(one, two, y, gate_weight[0], up_weight[0], down_weight[0], ffn_gain)
    back = jnp.stack([one.reshape(N, cap, cols), two.reshape(N, cap, cols)], axis=1)
    back = lax.all_to_all(back.reshape(experts * cap, cols), "mdl", 0, 0, tiled=True)
    mixture = 0.0
    for j in range(TOP):
        chosen_rows = jnp.dot(taken[:, j].astype(bf16), back, preferred_element_type=f32)
        mixture = mixture + weights[:, j : j + 1] * chosen_rows
    layer_out = (hidden_one.astype(f32) + mixture).astype(bf16)
    return swap_xy(layer_out)


def solution(mesh):
    placed = (
        P("ctx", "mdl"),
        P("ctx", "mdl"),
        P("ctx", "mdl"),
        P("mdl", None, None),
        P("mdl"),
        P("mdl", "ctx"),
        P("ctx", "mdl"),
        P(),
        P("ctx", None),
        P("ctx", None),
        P("mdl", None, "ctx"),
        P("mdl", None, "ctx"),
        P("mdl", "ctx", None),
    )
    return jax.shard_map(
        per_device, mesh=mesh, in_specs=placed, out_specs=P("ctx", "mdl"), check_vma=False
    )
```

```python
import jax
import jax.numpy as jnp
from jax import lax
from jax.experimental import pallas as pl
from jax.experimental.pallas import tpu as pltpu
from jax.sharding import PartitionSpec as P

DH = 128
TOP = 2
N = 4

VMEM = 14 * 1024 * 1024

epsilon = 1e-06
f32 = jnp.float32
bf16 = jnp.bfloat16


def move_z(v, s):
    return lax.ppermute(v, "ctx", [(y * N + z, y * N + (z + s) % N) for y in range(N) for z in range(N)])


def move_y(v, s):
    return lax.ppermute(v, "ctx", [(y * N + z, (y + s) % N * N + z) for y in range(N) for z in range(N)])


def move_m(v, s, flip):
    return lax.ppermute(v, "mdl", [(x * 2 + c, (x + s) % N * 2 + (c ^ flip)) for x in range(N) for c in range(2)])


def swap_xy(v):
    return lax.ppermute(v, ("ctx", "mdl"), device_pairs(lambda y, z, x, c: (x, z, y, c)))


def device_pairs(to):
    pairs = []
    for y in range(N):
        for z in range(N):
            for x in range(N):
                for c in range(2):
                    ty, tz, tx, tc = to(y, z, x, c)
                    pairs.append(((y * N + z) * 2 * N + x * 2 + c, (ty * N + tz) * 2 * N + tx * 2 + tc))
    return pairs


def carried_state(span, prefix_state, y, z, beside):
    quarter = span.shape[0] // N
    span = span.astype(bf16)

    def cut(a, q):
        return lax.dynamic_slice_in_dim(a, q % N * quarter, quarter, axis=0)

    mine = [cut(span, z).astype(f32)]
    for s in (1, 2, 3):
        mine.append(move_z(cut(span, z + s), s).astype(f32))
    total = (mine[0] + mine[1] + mine[2] + mine[3]).astype(bf16)
    base = cut(prefix_state, z)
    for s in (1, 2, 3):
        base = base + jnp.where((y - s) % N < y, move_y(total, s).astype(f32), 0.0)
    out = []
    for r in range(N):
        target = (z + r) % N
        acc = base
        for s in range(N):
            acc = acc + jnp.where((z - s) % N < target, mine[s], 0.0)
        acc = acc.astype(bf16)
        out.append(acc if r == 0 else move_z(acc, r))
    out, beside = lax.optimization_barrier((out, beside))
    turned = jnp.concatenate([out[3], out[2], out[1], out[0], out[3], out[2], out[1]], axis=0)
    return lax.dynamic_slice_in_dim(turned, (3 - z) * quarter, N * quarter, axis=0), beside


def attention(queries, keys, values, prefix_state, out_gain, y, z, beside):
    rows = queries.shape[0]
    heads = queries.shape[1] // DH
    q = queries.reshape(rows, heads, DH)
    k = keys.reshape(rows, heads, DH)
    v = values.reshape(rows, heads, DH)
    span = jnp.einsum("thd,the->hde", k, v, preferred_element_type=f32)
    carried, beside = carried_state(span, prefix_state, y, z, beside)
    scores = jnp.einsum("thd,shd->hts", q, k, preferred_element_type=f32)
    causal = jnp.arange(rows)[:, None] >= jnp.arange(rows)[None, :]
    scores = jnp.where(causal[None], scores, 0.0).astype(bf16)
    intra = jnp.einsum("hts,shd->thd", scores, v, preferred_element_type=f32)
    inter = jnp.einsum("thd,hde->the", q, carried, preferred_element_type=f32)
    raw = intra + inter
    scale = lax.rsqrt(jnp.mean(raw * raw, axis=2, keepdims=True) + epsilon)
    attn = raw * scale * out_gain.astype(f32).reshape(heads, DH)
    return attn.astype(bf16).reshape(rows, heads * DH), *beside


def call(kernel, outs, at, operands, name, flops=0, scratch=()):
    vmem = pl.BlockSpec(memory_space=pltpu.VMEM)
    many = isinstance(outs, list)
    moved = sum(v.size * v.dtype.itemsize for v in list(operands) + (outs if many else [outs]))
    return pl.pallas_call(
        kernel,
        in_specs=[pl.BlockSpec(memory_space=pltpu.SMEM)] + [vmem] * len(operands),
        out_specs=[vmem] * len(outs) if many else vmem,
        out_shape=outs,
        scratch_shapes=list(scratch),
        compiler_params=pltpu.CompilerParams(vmem_limit_bytes=VMEM),
        cost_estimate=pl.CostEstimate(flops=int(flops), bytes_accessed=int(moved), transcendentals=0),
        name=name,
    )(at, *operands)


def shaped(shape, dtype=bf16):
    return jax.ShapeDtypeStruct(shape, dtype)


def turned(at, k):
    return (at + k) & (N - 1)


def span_of(index, size):
    return pl.ds(pl.multiple_of(index * size, size), size)


def product(a, b):
    return jnp.dot(a, b, preferred_element_type=f32)


def wide_sum(*parts):
    total = parts[0].astype(f32)
    for p in parts[1:]:
        total = total + p.astype(f32)
    return total


def keep_weights(expert, after):
    hidden, model = expert[2].shape
    width = model // (2 * N)
    main = hidden // 128 * 128

    def kernel(g_ref, u_ref, d_ref, _, gate_up, down, done):
        here = span_of(pl.program_id(0), width)
        if main:
            gate_up[:main, here] = g_ref[:main, :]
            gate_up[main : 2 * main, here] = u_ref[:main, :]
        if main < hidden:
            gate_up[2 * main : main + hidden, here] = g_ref[main:, :]
            gate_up[main + hidden :, here] = u_ref[main:, :]
        down[:, here] = d_ref[...]
        done[...] = jnp.zeros_like(done)

    block = pl.BlockSpec((hidden, width), lambda g: (0, g))
    vmem = pl.BlockSpec(memory_space=pltpu.VMEM)
    gate_up, down, done = pl.pallas_call(
        kernel,
        grid=(2 * N,),
        in_specs=[block] * 3 + [vmem],
        out_specs=[vmem] * 3,
        out_shape=[pltpu.VMEM((2 * hidden, model), bf16), pltpu.VMEM((hidden, model), bf16), shaped((8, 128))],
        compiler_params=pltpu.CompilerParams(vmem_limit_bytes=VMEM),
        cost_estimate=pl.CostEstimate(flops=0, bytes_accessed=12 * hidden * model, transcendentals=0),
        name="keep_weights",
    )(*[pltpu.with_memory_space_constraint(w, pltpu.HBM) for w in expert], after)
    return (
        pltpu.with_memory_space_constraint(gate_up, pltpu.VMEM),
        pltpu.with_memory_space_constraint(down, pltpu.VMEM),
        done,
    )


def project(at, blocks, w_full):
    rows, depth = blocks[0].shape
    cols = w_full.shape[1] // 2

    def kernel(at, *refs):
        w, given, kept = refs[N:]
        x = jnp.concatenate([refs[k][...] for k in range(N)], axis=0)
        res = product(x, w[...]).astype(bf16)

        @pl.when(pl.program_id(0) == 0)
        def _():
            given[...] = res

        @pl.when(pl.program_id(0) == 1)
        def _():
            kept[...] = res

    vmem = pl.BlockSpec(memory_space=pltpu.VMEM)
    return pl.pallas_call(
        kernel,
        grid_spec=pltpu.PrefetchScalarGridSpec(
            num_scalar_prefetch=1,
            grid=(2,),
            in_specs=[vmem] * N + [pl.BlockSpec((depth, cols), lambda g, at: (0, (at[3] + g + 1) & 1))],
            out_specs=[vmem] * 2,
        ),
        out_shape=[shaped((N * rows, cols))] * 2,
        compiler_params=pltpu.CompilerParams(vmem_limit_bytes=VMEM),
        name="project",
    )(at, *blocks, w_full)


def pair_sums(at, kept, got):
    rows, cols = kept.shape[0] // N, kept.shape[1]

    def kernel(at, a, b, *outs):
        for s in range(N):
            here = span_of(turned(at[0] - at[2], N - s), rows)
            outs[s][...] = wide_sum(a[here, :], b[here, :]).astype(bf16)

    return call(kernel, [shaped((rows, cols))] * N, at, [kept, got], "pair_sums")


def hidden_and_picked(at, parts, resid, placing):
    def kernel(at, a, b, c, d, r, pick_ref, hidden, picked):
        h = (r[...].astype(f32) + wide_sum(a[...], b[...], c[...], d[...])).astype(bf16)
        hidden[...] = h
        picked[...] = product(pick_ref[...], h).astype(bf16)

    outs = [shaped(resid.shape), shaped((placing.shape[0], resid.shape[1]))]
    return call(kernel, outs, at, [*parts, resid, placing], "hidden")


def down_columns(at, ahead):
    return [2 * turned(at[0], r) for r in ahead] + [2 * turned(at[0], j) + 1 for j in range(N)]


def gate_up(at, sums, first, second, weights, gain, w_down=None, after=()):
    hidden, width = weights.shape[0] // 2, weights.shape[1] // (2 * N)
    main = hidden // 128 * 128
    rows = first[0][1][0].shape[0] * len(first[0][1])
    quarter = rows // N
    chunks = [p for _, parts in first + second for p in parts]
    last = w_down is not None
    n_sums = 0 if sums is None else 2

    def kernel(at, *refs):
        refs = list(refs)
        held = [refs.pop(0) for _ in range(n_sums)]
        own = [refs.pop(0) for _ in chunks]
        gn, wgu = refs.pop(0), refs.pop(0)
        for _ in after:
            refs.pop(0)
        if last:
            wd, inner, p_a, p_b, q_a, q_b, acc, acc_sq = refs
        else:
            acc, acc_sq = refs
        columns = [2 * turned(at[0], N - k) for k, _ in first] + [2 * turned(at[0], N - j) + 1 for j in range(N)]

        def products(pieces, i):
            w, column = wgu[:, span_of(columns[i], width)], columns[i]
            x = jnp.concatenate(pieces, axis=0)
            wide = x.astype(f32)
            sq = jnp.sum(wide * wide, axis=1, keepdims=True)
            new = lax.dot_general(x * gn[column], w, (((1,), (1,)), ((), ())), preferred_element_type=f32)
            return new, jnp.broadcast_to(sq, (x.shape[0], 128))

        taken = 0
        for n, (k, parts) in enumerate(first):
            pieces = [r[...] for r in own[taken : taken + len(parts)]]
            taken += len(parts)
            new, sq = products(pieces, n)
            if n > 0:
                acc[...] += new
                acc_sq[...] += sq
            elif n_sums:
                acc[...] = held[0][...] + new
                acc_sq[...] = held[1][...] + sq
            else:
                acc[...] = new
                acc_sq[...] = sq

        rest = []
        for k, parts in second:
            rest.append((k, own[taken : taken + len(parts)]))
            taken += len(parts)
        for j in range(N):
            pieces = []
            for k, mine in rest:
                per = N // len(mine)
                pieces.append(mine[j // per][j % per * quarter : (j % per + 1) * quarter, :])
            new, sq = products(pieces, len(first) + j)
            for i, (k, _) in enumerate(rest):
                to, part = slice(k * quarter, (k + 1) * quarter), slice(i * quarter, (i + 1) * quarter)
                acc[to, :] += new[part]
                acc_sq[to, :] += sq[part]

        if last:
            scale = lax.rsqrt(acc_sq[:, :1] / (2 * N * width) + epsilon)

            def silu(gate, up):
                gate = gate * scale
                return (gate / (1.0 + jnp.exp(-gate)) * (up * scale)).astype(bf16)

            if main:
                inner[:, :main] = silu(acc[:, :main], acc[:, main : 2 * main])
            if main < hidden:
                inner[:, main:] = silu(acc[:, 2 * main : main + hidden], acc[:, main + hidden :])
            res = product(inner[...], wd[:, span_of(2 * turned(at[0], 2), width)]).astype(bf16)
            p_a[...] = res[: rows // 2]
            p_b[...] = res[rows // 2 :]
            for j in range(N):
                w = wd[:, span_of(2 * turned(at[0], j) + 1, width)]
                res = product(inner[2 * quarter : 3 * quarter, :], w).astype(bf16)
                (q_a, q_b)[j // 2][j % 2 * quarter : (j % 2 + 1) * quarter, :] = res

    wide, sq = shaped((rows, 2 * hidden), f32), shaped((rows, 128), f32)
    flops = 4 * hidden * width * rows * (len(first) + len(second))
    operands = [*(sums or ()), *chunks, gain.reshape(2 * N, 1, width), weights]
    if not last:
        return call(kernel, [wide, sq], at, [*operands, *after], "gate_up", 4 * flops)
    outs = [shaped((rows, hidden))] + [shaped((rows // 2, width))] * 4
    scratch = [pltpu.VMEM(wide.shape, f32), pltpu.VMEM(sq.shape, f32)]
    return call(kernel, outs, at, [*operands, w_down], "gate_up_down", 6 * flops, scratch)


def down(at, inner, w_down, ahead, halves):
    rows, hidden = inner.shape
    quarter = rows // N
    width = w_down.shape[1] // (2 * N)
    n = len(ahead)
    per = 2 if halves else 1

    def kernel(at, x, w, *outs):
        columns = down_columns(at, ahead)

        def put(which, start, res):
            size = rows // per
            for p in range(per):
                low, high = max(start, p * size), min(start + res.shape[0], (p + 1) * size)
                if low < high:
                    outs[which * per + p][low - p * size : high - p * size, :] = res[low - start : high - start]

        for i in range(n):
            put(i, 0, product(x[...], w[:, span_of(columns[i], width)]).astype(bf16))
        starts = [(N - r) % N * quarter for r in ahead]
        xs = jnp.concatenate([x[s : s + quarter, :] for s in starts], axis=0)
        for j in range(N):
            res = product(xs, w[:, span_of(columns[n + j], width)]).astype(bf16)
            for i in range(n):
                put(n + i, j * quarter, res[i * quarter : (i + 1) * quarter])

    outs = [shaped((rows // per, width))] * (2 * n * per)
    return call(kernel, outs, at, [inner, w_down], "down", 12 * rows * hidden * width * n)


def add_pairs(at, pairs):
    def kernel(at, *refs):
        n = len(pairs)
        for i in range(n):
            refs[2 * n + i][...] = wide_sum(refs[2 * i][...], refs[2 * i + 1][...]).astype(bf16)

    return call(kernel, [shaped(a.shape) for a, _ in pairs], at, [v for p in pairs for v in p], "add_pairs")


def sum_quarters(at, sets):
    rows, width = sets[0][0].shape
    quarter = rows // N

    def kernel(at, *refs):
        outs = refs[5 * len(sets) :]
        for n in range(len(sets)):
            own, a_low, a_high, b_low, b_high = refs[5 * n : 5 * n + 5]
            for i in range(N):
                a, b = (a_low, b_low) if i < N // 2 else (a_high, b_high)
                to = slice(i % 2 * quarter, (i % 2 + 1) * quarter)
                res = wide_sum(own[i * quarter : (i + 1) * quarter, :], a[to, :], b[to, :])
                outs[n * N + i][...] = res.astype(bf16)

    outs = [shaped((quarter, width))] * (N * len(sets))
    res = call(kernel, outs, at, [v for s in sets for v in s], "sum_quarters")
    return [res[n * N : (n + 1) * N] for n in range(len(sets))]


def sum_to_blocks(at, ones, twos):
    rows, width = ones[0].shape
    cap = rows // N

    def kernel(at, *refs):
        out = refs[2 * N]
        one = wide_sum(*[r[...] for r in refs[:N]]).astype(bf16)
        two = wide_sum(*[r[...] for r in refs[N : 2 * N]]).astype(bf16)
        for b in range(N):
            out[2 * b * cap : (2 * b + 1) * cap, :] = one[b * cap : (b + 1) * cap]
            out[(2 * b + 1) * cap : (2 * b + 2) * cap, :] = two[b * cap : (b + 1) * cap]

    return call(kernel, shaped((2 * rows, width)), at, [*ones, *twos], "sum_to_blocks")


def combine(at, outs, place, weights, hidden_one):
    rows, width = hidden_one.shape

    def kernel(at, o, where, w, h, out):
        slots = lax.broadcasted_iota(jnp.int32, (rows, o.shape[0]), 1)
        total = h[...].astype(f32)
        for j in range(TOP):
            taken = jnp.where(where[:, j : j + 1] == slots, 1.0, 0.0).astype(bf16)
            total = total + w[:, j : j + 1] * product(taken, o[...])
        out[...] = total.astype(bf16)

    return call(kernel, shaped((rows, width)), at, [outs, place, weights, hidden_one], "combine")


def experts_out(at, one, two, expert, gain):
    ones = [one] + [move_z(one, s) for s in (1, 2, 3)]
    twos = [two] + [move_y(two, s) for s in (1, 2, 3)]
    weights, w_down, done = keep_weights(expert, one)
    ones, twos, done = lax.optimization_barrier((ones, twos, done))
    a_low, a_high = jnp.concatenate(ones[:2], axis=0), jnp.concatenate(ones[2:], axis=0)
    b_low, b_high = jnp.concatenate(twos[:2], axis=0), jnp.concatenate(twos[2:], axis=0)
    a1_low, a3_high = move_y(a_low, 1), move_y(a_high, -1)
    b1_low, b3_high = move_z(b_low, 1), move_z(b_high, -1)
    sums = gate_up(at, None, [(0, [a_low, a_high])], [(0, [b_low, b_high])], weights, gain, after=[done])
    sums, a_low, a_high, b_low, b_high, a1_low, a3_high, b1_low, b3_high = lax.optimization_barrier(
        (sums, a_low, a_high, b_low, b_high, a1_low, a3_high, b1_low, b3_high)
    )
    a1_high, a3_low = move_y(a_high, 1), move_y(a_low, -1)
    b1_high, b3_low = move_z(b_high, 1), move_z(b_low, -1)
    a2 = [move_y(a1_low, 1), move_y(a3_high, -1)]
    b2 = [move_z(b1_low, 1), move_z(b3_high, -1)]
    sums = gate_up(
        at,
        sums,
        [(1, [a1_low, a1_high]), (3, [a3_low, a3_high])],
        [(1, [b1_low, b1_high]), (3, [b3_low, b3_high])],
        weights,
        gain,
    )
    inner, p2a, p2b, q2a, q2b = gate_up(at, sums, [(2, a2)], [(2, b2)], weights, gain, w_down)
    p2a, p2b = move_y(p2a, 1), move_y(p2b, -1)
    q2a, q2b = move_z(q2a, 1), move_z(q2b, -1)
    p1a, p1b, p3a, p3b, q1a, q1b, q3a, q3b = down(at, inner, w_down, [1, 3], True)
    p1b, p3a = move_y(p1b, 1), move_y(p3a, -1)
    q1b, q3a = move_z(q1b, 1), move_z(q3a, -1)
    p1a, p3b, q1a, q3b = add_pairs(at, [(p1a, p2a), (p3b, p2b), (q1a, q2a), (q3b, q2b)])
    p1a, p3b = move_y(p1a, 1), move_y(p3b, -1)
    q1a, q3b = move_z(q1a, 1), move_z(q3b, -1)
    p0, q0 = down(at, inner, w_down, [0], False)
    p, q = sum_quarters(at, [(p0, p1a, p1b, p3a, p3b), (q0, q1a, q1b, q3a, q3b)])
    p = [p[0]] + [move_z(p[N - r], r) for r in (1, 2, 3)]
    q = [q[0]] + [move_y(q[r], r) for r in (1, 2, 3)]
    return sum_to_blocks(at, p, q)


def per_device(
    queries,
    keys,
    values,
    prefix_state,
    out_gain,
    out_weight,
    resid,
    ffn_gain,
    expert_ids,
    route_weights,
    gate_weight,
    up_weight,
    down_weight,
):
    ctx, mdl = lax.axis_index("ctx"), lax.axis_index("mdl")
    y, z = ctx // N, ctx % N
    x, c = mdl // 2, mdl % 2
    rows = queries.shape[0]
    cols = resid.shape[1]
    experts = 2 * N
    cap = 3 * rows * TOP // (2 * experts)

    chosen = expert_ids[:, :, None] == jnp.arange(experts, dtype=jnp.int32)
    uses = jnp.sum(chosen.astype(jnp.int32), axis=1)
    slots = jnp.cumsum(uses, axis=0) - uses
    slot_of = jnp.sum(jnp.where(chosen, slots[:, None, :], 0), axis=2)
    high = lax.reduce_precision(route_weights, 8, 7)
    middle = lax.reduce_precision(route_weights - high, 8, 7)
    low = route_weights - high - middle
    routing = jnp.concatenate([expert_ids.astype(f32), slot_of.astype(f32), high, middle, low], axis=1)
    routing = jnp.pad(routing.astype(bf16), ((0, 0), (0, 128 - 5 * TOP)))
    own = swap_xy(jnp.concatenate([resid, routing], axis=1))
    groups_z = [[a * N + b for b in range(N)] for a in range(N)]
    w_full = lax.all_gather(out_weight, "ctx", axis=1, tiled=True, axis_index_groups=groups_z)
    attn, own = attention(queries, keys, values, prefix_state, out_gain, y, z, (own,))

    own_resid, routing = own[:, :cols], own[:, cols : cols + 5 * TOP].astype(f32)
    routing = [routing[:, i * TOP : (i + 1) * TOP] for i in range(5)]
    place = (routing[0] * cap + routing[1]).astype(jnp.int32)
    weights = routing[2] + routing[3] + routing[4]
    placing = jnp.any(place[:, :, None] == jnp.arange(experts * cap, dtype=jnp.int32), axis=1).astype(bf16).T

    at = jnp.stack([y, z, x, c]).astype(jnp.int32)
    blocks = [attn] + [move_y(attn, s) for s in (1, 2, 3)]
    given, kept = project(at, blocks, w_full)
    given = move_m(given, 0, 1)
    parts = pair_sums(at, kept, given)
    parts = [parts[0]] + [move_m(parts[s], s, 0) for s in (1, 2, 3)]
    hidden_one, picked = hidden_and_picked(at, parts, own_resid, placing)
    picked = lax.all_to_all(picked, "mdl", 0, 0, tiled=True).reshape(N, 2, cap, cols)
    one, two = picked[:, 0].reshape(N * cap, cols), picked[:, 1].reshape(N * cap, cols)
    expert = [jnp.swapaxes(gate_weight[0], 0, 1), jnp.swapaxes(up_weight[0], 0, 1), down_weight[0]]
    outs = experts_out(at, one, two, expert, ffn_gain)
    outs = lax.all_to_all(outs, "mdl", 0, 0, tiled=True)
    return swap_xy(combine(at, outs, place, weights, hidden_one))


def solution(mesh):
    placed = (
        P("ctx", "mdl"),
        P("ctx", "mdl"),
        P("ctx", "mdl"),
        P("mdl", None, None),
        P("mdl"),
        P("mdl", "ctx"),
        P("ctx", "mdl"),
        P(),
        P("ctx", None),
        P("ctx", None),
        P("mdl", None, "ctx"),
        P("mdl", None, "ctx"),
        P("mdl", "ctx", None),
    )
    return jax.shard_map(
        per_device, mesh=mesh, in_specs=placed, out_specs=P("ctx", "mdl"), check_vma=False
    )
```

```python
import jax
import jax.numpy as jnp
from jax import lax
from jax.experimental import pallas as pl
from jax.experimental.pallas import tpu as pltpu
from jax.sharding import PartitionSpec as P

DH = 128
TOP = 2
N = 4

VMEM = 14 * 1024 * 1024

epsilon = 1e-06
f32 = jnp.float32
bf16 = jnp.bfloat16


def move_z(v, s):
    return lax.ppermute(v, "ctx", [(y * N + z, y * N + (z + s) % N) for y in range(N) for z in range(N)])


def move_y(v, s):
    return lax.ppermute(v, "ctx", [(y * N + z, (y + s) % N * N + z) for y in range(N) for z in range(N)])


def move_m(v, s, flip):
    return lax.ppermute(v, "mdl", [(x * 2 + c, (x + s) % N * 2 + (c ^ flip)) for x in range(N) for c in range(2)])


def trade(v, t):
    return lax.ppermute(v, ("ctx", "mdl"), device_pairs(lambda y, z, x, c: (y, 2 * c + (t ^ z % 2), x, z // 2)))


def by_parity(z, a, b):
    return jnp.where(z % 2 == 0, a, b), jnp.where(z % 2 == 0, b, a)


def device_pairs(to):
    pairs = []
    for y in range(N):
        for z in range(N):
            for x in range(N):
                for c in range(2):
                    ty, tz, tx, tc = to(y, z, x, c)
                    pairs.append(((y * N + z) * 2 * N + x * 2 + c, (ty * N + tz) * 2 * N + tx * 2 + tc))
    return pairs


def call(kernel, outs, at, operands, name, flops=0, scratch=()):
    vmem = pl.BlockSpec(memory_space=pltpu.VMEM)
    many = isinstance(outs, list)
    moved = sum(v.size * v.dtype.itemsize for v in list(operands) + (outs if many else [outs]))
    return pl.pallas_call(
        kernel,
        in_specs=[pl.BlockSpec(memory_space=pltpu.SMEM)] + [vmem] * len(operands),
        out_specs=[vmem] * len(outs) if many else vmem,
        out_shape=outs,
        scratch_shapes=list(scratch),
        compiler_params=pltpu.CompilerParams(vmem_limit_bytes=VMEM),
        cost_estimate=pl.CostEstimate(flops=int(flops), bytes_accessed=int(moved), transcendentals=0),
        name=name,
    )(at, *operands)


def shaped(shape, dtype=bf16):
    return jax.ShapeDtypeStruct(shape, dtype)


def turned(at, k):
    return (at + k) & (N - 1)


def span_of(index, size):
    return pl.ds(pl.multiple_of(index * size, size), size)


def product(a, b):
    return jnp.dot(a, b, preferred_element_type=f32)


def wide_sum(*parts):
    total = parts[0].astype(f32)
    for p in parts[1:]:
        total = total + p.astype(f32)
    return total


def spans(at, keys, values):
    quarter = keys.shape[1] // (N * DH)

    def kernel(at, k, v, *outs):
        for s in range(N):
            for i in range(quarter):
                here = span_of(turned(at[1], s) * quarter + i, DH)
                state = lax.dot_general(k[:, here], v[:, here], (((0,), (0,)), ((), ())), preferred_element_type=f32)
                outs[s][i * DH : (i + 1) * DH, :] = state.astype(bf16)

    return call(kernel, [shaped((quarter * DH, DH))] * N, at, [keys, values], "spans")


def scores_of(at, queries, keys):
    rows, heads = queries.shape[0], queries.shape[1] // DH

    def kernel(at, q, k, out):
        t = lax.broadcasted_iota(jnp.int32, (rows, rows), 0)
        s = lax.broadcasted_iota(jnp.int32, (rows, rows), 1)
        for h in range(heads):
            here = slice(h * DH, (h + 1) * DH)
            res = lax.dot_general(q[:, here], k[:, here], (((1,), (1,)), ((), ())), preferred_element_type=f32)
            out[h] = jnp.where(s <= t, res, 0.0).astype(bf16)

    return call(kernel, shaped((heads, rows, rows)), at, [queries, keys], "scores")


def carried_states(span, prefix_state, y, z):
    rows = span[0].shape[0]
    mine = [span[0].astype(f32)] + [move_z(span[s], s).astype(f32) for s in (1, 2, 3)]
    total = (mine[0] + mine[1] + mine[2] + mine[3]).astype(bf16)
    base = lax.dynamic_slice_in_dim(prefix_state.reshape(N * rows, DH), z * rows, rows, axis=0)
    for s in (1, 2, 3):
        base = base + jnp.where((y - s) % N < y, move_y(total, s).astype(f32), 0.0)
    out = []
    for r in range(N):
        target = (z + r) % N
        acc = base
        for s in range(N):
            acc = acc + jnp.where((z - s) % N < target, mine[s], 0.0)
        acc = acc.astype(bf16)
        out.append(acc if r == 0 else move_z(acc, r))
    return out


def attend(at, queries, values, scores, carried, out_gain):
    quarter = queries.shape[1] // (N * DH)

    def kernel(at, q, v, sc, *refs):
        *states, gain, out = refs
        for r in range(N):
            for i in range(quarter):
                head = turned(at[1], N - r) * quarter + i
                here = span_of(head, DH)
                raw = product(sc[head], v[:, here]) + product(q[:, here], states[r][i * DH : (i + 1) * DH, :])
                scale = lax.rsqrt(jnp.mean(raw * raw, axis=1, keepdims=True) + epsilon)
                out[:, here] = (raw * scale * gain[head]).astype(bf16)

    gain = out_gain.astype(f32).reshape(-1, 1, DH)
    return call(kernel, shaped(queries.shape), at, [queries, values, scores, *carried, gain], "attend")


def keep_weights(expert, after):
    hidden, model = expert[2].shape
    width = model // (N * N)
    main = hidden // 128 * 128

    def kernel(*refs):
        gate_up, down, done = refs[7:]
        for i in range(2):
            g_ref, u_ref, d_ref = refs[i], refs[2 + i], refs[4 + i]
            here = span_of(2 * pl.program_id(0) + i, width)
            if main:
                gate_up[:main, here] = g_ref[:main, :]
                gate_up[main : 2 * main, here] = u_ref[:main, :]
            if main < hidden:
                gate_up[2 * main : main + hidden, here] = g_ref[main:, :]
                gate_up[main + hidden :, here] = u_ref[main:, :]
            down[:, here] = d_ref[...]
        done[...] = jnp.zeros_like(done)

    blocks = [pl.BlockSpec((hidden, width), lambda g, i=i: (0, N * (2 * (g % 2) + i) + g // 2)) for i in range(2)]
    vmem = pl.BlockSpec(memory_space=pltpu.VMEM)
    gate_up, down, done = pl.pallas_call(
        kernel,
        grid=(2 * N,),
        in_specs=blocks * 3 + [vmem],
        out_specs=[vmem] * 3,
        out_shape=[pltpu.VMEM((2 * hidden, model), bf16), pltpu.VMEM((hidden, model), bf16), shaped((8, 128))],
        compiler_params=pltpu.CompilerParams(vmem_limit_bytes=VMEM),
        cost_estimate=pl.CostEstimate(flops=0, bytes_accessed=12 * hidden * model, transcendentals=0),
        name="keep_weights",
    )(*[pltpu.with_memory_space_constraint(w, pltpu.HBM) for w in expert for _ in range(2)], after)
    return (
        pltpu.with_memory_space_constraint(gate_up, pltpu.VMEM),
        pltpu.with_memory_space_constraint(down, pltpu.VMEM),
        done,
    )


def project(at, blocks, w_full):
    rows, depth = blocks[0].shape
    cols = w_full.shape[1] // 2

    def kernel(at, *refs):
        w, given, kept, x = refs[N:]
        here = span_of(pl.program_id(0), cols)

        @pl.when(pl.program_id(0) == 0)
        def _():
            for k in range(N):
                x[span_of(turned(at[1], N - k), rows), :] = refs[k][...]

        given[:, here] = product(x[span_of(1 - at[3], 2 * rows), :], w[...]).astype(bf16)
        kept[:, here] = product(x[span_of(at[3], 2 * rows), :], w[...]).astype(bf16)

    vmem = pl.BlockSpec(memory_space=pltpu.VMEM)
    return pl.pallas_call(
        kernel,
        grid_spec=pltpu.PrefetchScalarGridSpec(
            num_scalar_prefetch=1,
            grid=(2,),
            in_specs=[vmem] * N + [pl.BlockSpec((depth, cols), lambda g, at: (0, g))],
            out_specs=[vmem] * 2,
            scratch_shapes=[pltpu.VMEM((N * rows, depth), bf16)],
        ),
        out_shape=[shaped((2 * rows, 2 * cols))] * 2,
        compiler_params=pltpu.CompilerParams(vmem_limit_bytes=VMEM),
        name="project",
    )(at, *blocks, pltpu.with_memory_space_constraint(w_full, pltpu.HBM))


def pair_sums(at, kept, got):
    rows, cols = kept.shape[0], kept.shape[1] // N

    def kernel(at, a, b, *outs):
        for s in range(N):
            here = span_of(turned(at[2], s), cols)
            outs[s][...] = wide_sum(a[:, here], b[:, here]).astype(bf16)

    return call(kernel, [shaped((rows, cols))] * N, at, [kept, got], "pair_sums")


def hidden_and_picked(at, parts, resid, placing):
    def kernel(at, a, b, c, d, r, pick_ref, hidden, picked):
        h = (r[...].astype(f32) + wide_sum(a[...], b[...], c[...], d[...])).astype(bf16)
        hidden[...] = h
        picked[...] = product(pick_ref[...], h).astype(bf16)

    outs = [shaped(resid.shape), shaped((placing.shape[0], resid.shape[1]))]
    return call(kernel, outs, at, [*parts, resid, placing], "hidden")


def down_columns(at, ahead):
    return [2 * turned(at[1], r) for r in ahead] + [2 * turned(at[1], j) + 1 for j in range(N)]


def gate_up(at, sums, first, second, weights, gain, w_down=None, after=()):
    hidden, width = weights.shape[0] // 2, weights.shape[1] // (2 * N)
    main = hidden // 128 * 128
    rows = first[0][1][0].shape[0] * len(first[0][1])
    quarter = rows // N
    chunks = [p for _, parts in first + second for p in parts]
    last = w_down is not None
    n_sums = 0 if sums is None else 2

    def kernel(at, *refs):
        refs = list(refs)
        held = [refs.pop(0) for _ in range(n_sums)]
        own = [refs.pop(0) for _ in chunks]
        gn, wgu = refs.pop(0), refs.pop(0)
        for _ in after:
            refs.pop(0)
        if last:
            wd, inner, p_a, p_b, q_a, q_b, acc, acc_sq = refs
        else:
            acc, acc_sq = refs
        columns = [2 * turned(at[1], N - k) for k, _ in first] + [2 * turned(at[1], N - j) + 1 for j in range(N)]

        def products(pieces, i):
            w, column = wgu[:, span_of(columns[i], width)], columns[i]
            x = jnp.concatenate(pieces, axis=0)
            wide = x.astype(f32)
            sq = jnp.sum(wide * wide, axis=1, keepdims=True)
            new = lax.dot_general(x * gn[column], w, (((1,), (1,)), ((), ())), preferred_element_type=f32)
            return new, jnp.broadcast_to(sq, (x.shape[0], 128))

        taken = 0
        for n, (k, parts) in enumerate(first):
            pieces = [r[...] for r in own[taken : taken + len(parts)]]
            taken += len(parts)
            new, sq = products(pieces, n)
            if n > 0:
                acc[...] += new
                acc_sq[...] += sq
            elif n_sums:
                acc[...] = held[0][...] + new
                acc_sq[...] = held[1][...] + sq
            else:
                acc[...] = new
                acc_sq[...] = sq

        rest = []
        for k, parts in second:
            rest.append((k, own[taken : taken + len(parts)]))
            taken += len(parts)
        for j in range(N):
            pieces = []
            for k, mine in rest:
                per = N // len(mine)
                pieces.append(mine[j // per][j % per * quarter : (j % per + 1) * quarter, :])
            new, sq = products(pieces, len(first) + j)
            for i, (k, _) in enumerate(rest):
                to, part = slice(k * quarter, (k + 1) * quarter), slice(i * quarter, (i + 1) * quarter)
                acc[to, :] += new[part]
                acc_sq[to, :] += sq[part]

        if last:
            scale = lax.rsqrt(acc_sq[:, :1] / (2 * N * width) + epsilon)

            def silu(gate, up):
                gate = gate * scale
                return (gate / (1.0 + jnp.exp(-gate)) * (up * scale)).astype(bf16)

            if main:
                inner[:, :main] = silu(acc[:, :main], acc[:, main : 2 * main])
            if main < hidden:
                inner[:, main:] = silu(acc[:, 2 * main : main + hidden], acc[:, main + hidden :])
            res = product(inner[...], wd[:, span_of(2 * turned(at[1], 2), width)]).astype(bf16)
            p_a[...] = res[: rows // 2]
            p_b[...] = res[rows // 2 :]
            for j in range(N):
                w = wd[:, span_of(2 * turned(at[1], j) + 1, width)]
                res = product(inner[2 * quarter : 3 * quarter, :], w).astype(bf16)
                (q_a, q_b)[j // 2][j % 2 * quarter : (j % 2 + 1) * quarter, :] = res

    wide, sq = shaped((rows, 2 * hidden), f32), shaped((rows, 128), f32)
    flops = 4 * hidden * width * rows * (len(first) + len(second))
    operands = [*(sums or ()), *chunks, gain.reshape(N, N, -1).swapaxes(0, 1).reshape(2 * N, 1, width), weights]
    if not last:
        return call(kernel, [wide, sq], at, [*operands, *after], "gate_up", 4 * flops)
    outs = [shaped((rows, hidden))] + [shaped((rows // 2, width))] * 4
    scratch = [pltpu.VMEM(wide.shape, f32), pltpu.VMEM(sq.shape, f32)]
    return call(kernel, outs, at, [*operands, w_down], "gate_up_down", 6 * flops, scratch)


def down(at, inner, w_down, ahead, halves):
    rows, hidden = inner.shape
    quarter = rows // N
    width = w_down.shape[1] // (2 * N)
    n = len(ahead)
    per = 2 if halves else 1

    def kernel(at, x, w, *outs):
        columns = down_columns(at, ahead)

        def put(which, start, res):
            size = rows // per
            for p in range(per):
                low, high = max(start, p * size), min(start + res.shape[0], (p + 1) * size)
                if low < high:
                    outs[which * per + p][low - p * size : high - p * size, :] = res[low - start : high - start]

        for i in range(n):
            put(i, 0, product(x[...], w[:, span_of(columns[i], width)]).astype(bf16))
        starts = [(N - r) % N * quarter for r in ahead]
        xs = jnp.concatenate([x[s : s + quarter, :] for s in starts], axis=0)
        for j in range(N):
            res = product(xs, w[:, span_of(columns[n + j], width)]).astype(bf16)
            for i in range(n):
                put(n + i, j * quarter, res[i * quarter : (i + 1) * quarter])

    outs = [shaped((rows // per, width))] * (2 * n * per)
    return call(kernel, outs, at, [inner, w_down], "down", 12 * rows * hidden * width * n)


def add_pairs(at, pairs):
    def kernel(at, *refs):
        n = len(pairs)
        for i in range(n):
            refs[2 * n + i][...] = wide_sum(refs[2 * i][...], refs[2 * i + 1][...]).astype(bf16)

    return call(kernel, [shaped(a.shape) for a, _ in pairs], at, [v for p in pairs for v in p], "add_pairs")


def sum_quarters(at, sets):
    rows, width = sets[0][0].shape
    quarter = rows // N

    def kernel(at, *refs):
        outs = refs[5 * len(sets) :]
        for n in range(len(sets)):
            own, a_low, a_high, b_low, b_high = refs[5 * n : 5 * n + 5]
            for i in range(N):
                a, b = (a_low, b_low) if i < N // 2 else (a_high, b_high)
                to = slice(i % 2 * quarter, (i % 2 + 1) * quarter)
                res = wide_sum(own[i * quarter : (i + 1) * quarter, :], a[to, :], b[to, :])
                outs[n * N + i][...] = res.astype(bf16)

    outs = [shaped((quarter, width))] * (N * len(sets))
    res = call(kernel, outs, at, [v for s in sets for v in s], "sum_quarters")
    return [res[n * N : (n + 1) * N] for n in range(len(sets))]


def sum_to_blocks(at, ones, twos):
    rows, width = ones[0].shape
    half, cols = rows // 2, width // 2

    def kernel(at, *refs):
        out = refs[2 * N]
        one = wide_sum(*[r[...] for r in refs[:N]]).astype(bf16)
        two = wide_sum(*[r[...] for r in refs[N : 2 * N]]).astype(bf16)
        for x in range(N):
            part = (one, two)[x // 2][:, x % 2 * cols : (x % 2 + 1) * cols]
            out[x * rows : (x + 1) * rows, :] = part

    return call(kernel, shaped((N * rows, cols)), at, [*ones, *twos], "sum_to_blocks")


def combine(at, outs, place, weights, hidden_one):
    rows, width = hidden_one.shape

    def kernel(at, o, where, w, h, first, second):
        slots = lax.broadcasted_iota(jnp.int32, (rows, o.shape[0]), 1)
        total = h[...].astype(f32)
        for j in range(TOP):
            taken = jnp.where(where[:, j : j + 1] == slots, 1.0, 0.0).astype(bf16)
            total = total + w[:, j : j + 1] * product(taken, o[...])
        total = total.astype(bf16)
        low, high = total[: rows // 2], total[rows // 2 :]
        even = (at[1] & 1) == 0
        first[...] = jnp.where(even, low, high)
        second[...] = jnp.where(even, high, low)

    return call(kernel, [shaped((rows // 2, width))] * 2, at, [outs, place, weights, hidden_one], "combine")


def experts_out(at, one, two, expert, gain):
    ones = [one] + [move_y(one, s) for s in (1, 2, 3)]
    twos = [two] + [move_z(two, s) for s in (1, 2, 3)]
    weights, w_down, done = keep_weights(expert, one)
    ones, twos, done = lax.optimization_barrier((ones, twos, done))
    a_low, a_high = jnp.concatenate(ones[:2], axis=0), jnp.concatenate(ones[2:], axis=0)
    b_low, b_high = jnp.concatenate(twos[:2], axis=0), jnp.concatenate(twos[2:], axis=0)
    a1_low, a3_high = move_z(a_low, 1), move_z(a_high, -1)
    b1_low, b3_high = move_y(b_low, 1), move_y(b_high, -1)
    sums = gate_up(at, None, [(0, [a_low, a_high])], [(0, [b_low, b_high])], weights, gain, after=[done])
    sums, a_low, a_high, b_low, b_high, a1_low, a3_high, b1_low, b3_high = lax.optimization_barrier(
        (sums, a_low, a_high, b_low, b_high, a1_low, a3_high, b1_low, b3_high)
    )
    a1_high, a3_low = move_z(a_high, 1), move_z(a_low, -1)
    b1_high, b3_low = move_y(b_high, 1), move_y(b_low, -1)
    a2 = [move_z(a1_low, 1), move_z(a3_high, -1)]
    b2 = [move_y(b1_low, 1), move_y(b3_high, -1)]
    sums = gate_up(
        at,
        sums,
        [(1, [a1_low, a1_high]), (3, [a3_low, a3_high])],
        [(1, [b1_low, b1_high]), (3, [b3_low, b3_high])],
        weights,
        gain,
    )
    inner, p2a, p2b, q2a, q2b = gate_up(at, sums, [(2, a2)], [(2, b2)], weights, gain, w_down)
    p2a, p2b = move_z(p2a, 1), move_z(p2b, -1)
    q2a, q2b = move_y(q2a, 1), move_y(q2b, -1)
    p1a, p1b, p3a, p3b, q1a, q1b, q3a, q3b = down(at, inner, w_down, [1, 3], True)
    p1b, p3a = move_z(p1b, 1), move_z(p3a, -1)
    q1b, q3a = move_y(q1b, 1), move_y(q3a, -1)
    p1a, p3b, q1a, q3b = add_pairs(at, [(p1a, p2a), (p3b, p2b), (q1a, q2a), (q3b, q2b)])
    p1a, p3b = move_z(p1a, 1), move_z(p3b, -1)
    q1a, q3b = move_y(q1a, 1), move_y(q3b, -1)
    p0, q0 = down(at, inner, w_down, [0], False)
    p, q = sum_quarters(at, [(p0, p1a, p1b, p3a, p3b), (q0, q1a, q1b, q3a, q3b)])
    p = [p[0]] + [move_y(p[N - r], r) for r in (1, 2, 3)]
    q = [q[0]] + [move_z(q[r], r) for r in (1, 2, 3)]
    return sum_to_blocks(at, p, q)


def per_device(
    queries,
    keys,
    values,
    prefix_state,
    out_gain,
    out_weight,
    resid,
    ffn_gain,
    expert_ids,
    route_weights,
    gate_weight,
    up_weight,
    down_weight,
):
    ctx, mdl = lax.axis_index("ctx"), lax.axis_index("mdl")
    y, z = ctx // N, ctx % N
    x, c = mdl // 2, mdl % 2
    rows = queries.shape[0]
    cols = resid.shape[1]
    experts = 2 * N
    cap = 3 * rows * TOP // (2 * experts)

    chosen = expert_ids[:, :, None] == jnp.arange(experts, dtype=jnp.int32)
    uses = jnp.sum(chosen.astype(jnp.int32), axis=1)
    slots = jnp.cumsum(uses, axis=0) - uses
    slot_of = jnp.sum(jnp.where(chosen, slots[:, None, :], 0), axis=2)
    high = lax.reduce_precision(route_weights, 8, 7)
    middle = lax.reduce_precision(route_weights - high, 8, 7)
    low = route_weights - high - middle
    routing = jnp.concatenate([expert_ids.astype(f32), slot_of.astype(f32), high, middle, low], axis=1)
    routing = jnp.pad(routing.astype(bf16), ((0, 0), (0, 128 - 5 * TOP)))
    half = cols // 2
    own = by_parity(z, resid[:, :half], resid[:, half:])
    own = [jnp.concatenate([part, routing], axis=1) for part in own]
    groups_y = [[a * N + b for a in range(N)] for b in range(N)]
    w_full = lax.all_gather(out_weight, "ctx", axis=1, tiled=True, axis_index_groups=groups_y)
    at = jnp.stack([y, z, x, c]).astype(jnp.int32)
    carried = carried_states(spans(at, keys, values), prefix_state, y, z)
    attn = attend(at, queries, values, scores_of(at, queries, keys), carried, out_gain)

    blocks = [attn] + [move_z(attn, s) for s in (1, 2, 3)]
    blocks[1], own = lax.optimization_barrier((blocks[1], own))
    own = by_parity(z, trade(own[0], 0), trade(own[1], 1))
    own = jnp.concatenate(own, axis=0)
    own_resid, routing = own[:, :half], own[:, half : half + 5 * TOP].astype(f32)
    routing = [routing[:, i * TOP : (i + 1) * TOP] for i in range(5)]
    block = jnp.repeat(jnp.arange(2, dtype=jnp.int32), rows)[:, None] * cap
    place = (routing[0] * (2 * cap) + routing[1]).astype(jnp.int32) + block
    weights = routing[2] + routing[3] + routing[4]
    placing = jnp.any(place[:, :, None] == jnp.arange(2 * experts * cap, dtype=jnp.int32), axis=1).astype(bf16).T
    given, kept = project(at, blocks, w_full)
    given = move_m(given, 0, 1)
    parts = pair_sums(at, kept, given)
    parts = [parts[0]] + [move_m(parts[s], s, 0) for s in (1, 2, 3)]
    hidden_one, picked = hidden_and_picked(at, parts, own_resid, placing)
    picked = lax.all_to_all(picked, "mdl", 0, 0, tiled=True).reshape(2, 2, 2, 2 * cap, half)
    one, two = [picked[h].transpose(1, 2, 0, 3).reshape(N * cap, cols) for h in range(2)]
    expert = [jnp.swapaxes(gate_weight[0], 0, 1), jnp.swapaxes(up_weight[0], 0, 1), down_weight[0]]
    outs = experts_out(at, one, two, expert, ffn_gain)
    outs = lax.all_to_all(outs, "mdl", 0, 0, tiled=True)
    first, second = combine(at, outs, place, weights, hidden_one)
    return jnp.concatenate(by_parity(z, trade(first, 0), trade(second, 1)), axis=1)


def solution(mesh):
    placed = (
        P("ctx", "mdl"),
        P("ctx", "mdl"),
        P("ctx", "mdl"),
        P("mdl", None, None),
        P("mdl"),
        P("mdl", "ctx"),
        P("ctx", "mdl"),
        P(),
        P("ctx", None),
        P("ctx", None),
        P("mdl", None, "ctx"),
        P("mdl", None, "ctx"),
        P("mdl", "ctx", None),
    )
    return jax.shard_map(
        per_device, mesh=mesh, in_specs=placed, out_specs=P("ctx", "mdl"), check_vma=False
    )
```

```python
import jax
import jax.numpy as jnp
from jax import lax
from jax.experimental import pallas as pl
from jax.experimental.pallas import tpu as pltpu
from jax.sharding import PartitionSpec as P

DH = 128
TOP = 2
N = 4

VMEM = 8 * 1024 * 1024

epsilon = 1e-06
f32 = jnp.float32
bf16 = jnp.bfloat16


def move_z(v, s):
    return lax.ppermute(v, "ctx", [(y * N + z, y * N + (z + s) % N) for y in range(N) for z in range(N)])


def move_y(v, s):
    return lax.ppermute(v, "ctx", [(y * N + z, (y + s) % N * N + z) for y in range(N) for z in range(N)])


def move_m(v, s, flip):
    return lax.ppermute(v, "mdl", [(x * 2 + c, (x + s) % N * 2 + (c ^ flip)) for x in range(N) for c in range(2)])


def trade(v, t):
    return lax.ppermute(v, ("ctx", "mdl"), device_pairs(lambda y, z, x, c: (y, 2 * c + (t ^ z % 2), x, z // 2)))


def by_parity(z, a, b):
    return jnp.where(z % 2 == 0, a, b), jnp.where(z % 2 == 0, b, a)


def device_pairs(to):
    pairs = []
    for y in range(N):
        for z in range(N):
            for x in range(N):
                for c in range(2):
                    ty, tz, tx, tc = to(y, z, x, c)
                    pairs.append(((y * N + z) * 2 * N + x * 2 + c, (ty * N + tz) * 2 * N + tx * 2 + tc))
    return pairs


def call(kernel, outs, at, operands, name, flops=0, scratch=()):
    vmem = pl.BlockSpec(memory_space=pltpu.VMEM)
    many = isinstance(outs, list)
    moved = sum(v.size * v.dtype.itemsize for v in list(operands) + (outs if many else [outs]))
    return pl.pallas_call(
        kernel,
        in_specs=[pl.BlockSpec(memory_space=pltpu.SMEM)] + [vmem] * len(operands),
        out_specs=[vmem] * len(outs) if many else vmem,
        out_shape=outs,
        scratch_shapes=list(scratch),
        compiler_params=pltpu.CompilerParams(vmem_limit_bytes=VMEM),
        cost_estimate=pl.CostEstimate(flops=int(flops), bytes_accessed=int(moved), transcendentals=0),
        name=name,
    )(at, *operands)


def shaped(shape, dtype=bf16):
    return jax.ShapeDtypeStruct(shape, dtype)


def turned(at, k):
    return (at + k) & (N - 1)


def span_of(index, size):
    return pl.ds(pl.multiple_of(index * size, size), size)


def product(a, b):
    return jnp.dot(a, b, preferred_element_type=f32)


def wide_sum(*parts):
    total = parts[0].astype(f32)
    for p in parts[1:]:
        total = total + p.astype(f32)
    return total


def spans(at, keys, values):
    quarter = keys.shape[1] // (N * DH)

    def kernel(at, k, v, *outs):
        for s in range(N):
            for i in range(quarter):
                here = span_of(turned(at[1], s) * quarter + i, DH)
                state = lax.dot_general(k[:, here], v[:, here], (((0,), (0,)), ((), ())), preferred_element_type=f32)
                outs[s][i * DH : (i + 1) * DH, :] = state.astype(bf16)

    whole = pl.BlockSpec(keys.shape, lambda g, at: (0, 0))
    vmem = pl.BlockSpec(memory_space=pltpu.VMEM)
    return pl.pallas_call(
        kernel,
        grid_spec=pltpu.PrefetchScalarGridSpec(
            num_scalar_prefetch=1, grid=(1,), in_specs=[whole] * 2, out_specs=[vmem] * N
        ),
        out_shape=[shaped((quarter * DH, DH))] * N,
        compiler_params=pltpu.CompilerParams(vmem_limit_bytes=VMEM),
        name="spans",
    )(at, *[pltpu.with_memory_space_constraint(v, pltpu.HBM) for v in (keys, values)])


def scores_of(at, queries, keys):
    rows, heads = queries.shape[0], queries.shape[1] // DH

    def kernel(at, q, k, out):
        t = lax.broadcasted_iota(jnp.int32, (rows, rows), 0)
        s = lax.broadcasted_iota(jnp.int32, (rows, rows), 1)
        for h in range(heads):
            here = slice(h * DH, (h + 1) * DH)
            res = lax.dot_general(q[:, here], k[:, here], (((1,), (1,)), ((), ())), preferred_element_type=f32)
            out[h] = jnp.where(s <= t, res, 0.0).astype(bf16)

    return call(kernel, shaped((heads, rows, rows)), at, [queries, keys], "scores")


def carried_states(span, prefix_state, y, z):
    rows = span[0].shape[0]
    mine = [span[0].astype(f32)] + [move_z(span[s], s).astype(f32) for s in (1, 2, 3)]
    total = (mine[0] + mine[1] + mine[2] + mine[3]).astype(bf16)
    base = lax.dynamic_slice_in_dim(prefix_state.reshape(N * rows, DH), z * rows, rows, axis=0)
    for s in (1, 2, 3):
        base = base + jnp.where((y - s) % N < y, move_y(total, s).astype(f32), 0.0)
    out = []
    for r in range(N):
        target = (z + r) % N
        acc = base
        for s in range(N):
            acc = acc + jnp.where((z - s) % N < target, mine[s], 0.0)
        acc = acc.astype(bf16)
        out.append(acc if r == 0 else move_z(acc, r))
    return out


def attend(at, queries, values, scores, carried, out_gain):
    quarter = queries.shape[1] // (N * DH)

    def kernel(at, q, v, sc, *refs):
        *states, gain, out = refs
        for r in range(N):
            for i in range(quarter):
                head = turned(at[1], N - r) * quarter + i
                here = span_of(head, DH)
                raw = product(sc[head], v[:, here]) + product(q[:, here], states[r][i * DH : (i + 1) * DH, :])
                scale = lax.rsqrt(jnp.mean(raw * raw, axis=1, keepdims=True) + epsilon)
                out[:, here] = (raw * scale * gain[head]).astype(bf16)

    gain = out_gain.astype(f32).reshape(-1, 1, DH)
    return call(kernel, shaped(queries.shape), at, [queries, values, scores, *carried, gain], "attend")


def keep_weights(expert, after):
    hidden, model = expert[0].shape
    width = model // (N * N)
    main = hidden // 128 * 128

    def kernel(*refs):
        gate_up, done = refs[5:]
        for i in range(2):
            g_ref, u_ref = refs[i], refs[2 + i]
            here = span_of(2 * pl.program_id(0) + i, width)
            if main:
                gate_up[:main, here] = g_ref[:main, :]
                gate_up[main : 2 * main, here] = u_ref[:main, :]
            if main < hidden:
                gate_up[2 * main : main + hidden, here] = g_ref[main:, :]
                gate_up[main + hidden :, here] = u_ref[main:, :]
        done[...] = jnp.zeros_like(done)

    blocks = [pl.BlockSpec((hidden, width), lambda g, i=i: (0, N * (2 * (g % 2) + i) + g // 2)) for i in range(2)]
    vmem = pl.BlockSpec(memory_space=pltpu.VMEM)
    gate_up, done = pl.pallas_call(
        kernel,
        grid=(2 * N,),
        in_specs=blocks * 2 + [vmem],
        out_specs=[vmem] * 2,
        out_shape=[pltpu.VMEM((2 * hidden, model), bf16), shaped((8, 128))],
        compiler_params=pltpu.CompilerParams(vmem_limit_bytes=VMEM),
        cost_estimate=pl.CostEstimate(flops=0, bytes_accessed=8 * hidden * model, transcendentals=0),
        name="keep_weights",
    )(*[pltpu.with_memory_space_constraint(w, pltpu.HBM) for w in expert for _ in range(2)], after)
    return pltpu.with_memory_space_constraint(gate_up, pltpu.VMEM), done


def project(at, blocks, w_full):
    rows, depth = blocks[0].shape
    cols = w_full.shape[1] // 2

    def kernel(at, *refs):
        w, given, kept, x, res = refs[N:]
        here = span_of(pl.program_id(0), cols)

        @pl.when(pl.program_id(0) == 0)
        def _():
            for k in range(N):
                x[span_of(turned(at[1], N - k), rows), :] = refs[k][...]

        res[...] = product(x[...], w[...]).astype(bf16)
        given[:, here] = res[span_of(1 - at[3], 2 * rows), :]
        kept[:, here] = res[span_of(at[3], 2 * rows), :]

    vmem = pl.BlockSpec(memory_space=pltpu.VMEM)
    return pl.pallas_call(
        kernel,
        grid_spec=pltpu.PrefetchScalarGridSpec(
            num_scalar_prefetch=1,
            grid=(2,),
            in_specs=[vmem] * N + [pl.BlockSpec((depth, cols), lambda g, at: (0, g))],
            out_specs=[vmem] * 2,
            scratch_shapes=[pltpu.VMEM((N * rows, depth), bf16), pltpu.VMEM((N * rows, cols), bf16)],
        ),
        out_shape=[shaped((2 * rows, 2 * cols))] * 2,
        compiler_params=pltpu.CompilerParams(vmem_limit_bytes=VMEM),
        name="project",
    )(at, *blocks, pltpu.with_memory_space_constraint(w_full, pltpu.HBM))


def pair_sums(at, kept, got):
    rows, cols = kept.shape[0], kept.shape[1] // N

    def kernel(at, a, b, *outs):
        for s in range(N):
            here = span_of(turned(at[2], s), cols)
            outs[s][...] = wide_sum(a[:, here], b[:, here]).astype(bf16)

    return call(kernel, [shaped((rows, cols))] * N, at, [kept, got], "pair_sums")


def hidden_and_picked(at, parts, resid, placing):
    def kernel(at, a, b, c, d, r, pick_ref, hidden, picked):
        h = (r[...].astype(f32) + wide_sum(a[...], b[...], c[...], d[...])).astype(bf16)
        hidden[...] = h
        picked[...] = product(pick_ref[...], h).astype(bf16)

    outs = [shaped(resid.shape), shaped((placing.shape[0], resid.shape[1]))]
    return call(kernel, outs, at, [*parts, resid, placing], "hidden")


def down_block(w, z, h, width):
    return jnp.concatenate([w[:, span_of(N * (2 * h + i) + z, width // 2)] for i in range(2)], axis=1)


def gate_up(at, sums, first, second, weights, gain, w_down=None, after=()):
    hidden, width = weights.shape[0] // 2, weights.shape[1] // (2 * N)
    main = hidden // 128 * 128
    rows = first[0][1][0].shape[0] * len(first[0][1])
    quarter = rows // N
    chunks = [p for _, parts in first + second for p in parts]
    last = w_down is not None
    n_sums = 0 if sums is None else 2

    def kernel(at, *refs):
        refs = list(refs)
        held = [refs.pop(0) for _ in range(n_sums)]
        own = [refs.pop(0) for _ in chunks]
        gn, wgu = refs.pop(0), refs.pop(0)
        for _ in after:
            refs.pop(0)
        if last:
            wd, inner, p_a, p_b, q_a, q_b, acc, acc_sq = refs
        else:
            acc, acc_sq = refs
        columns = [2 * turned(at[1], N - k) for k, _ in first] + [2 * turned(at[1], N - j) + 1 for j in range(N)]

        def products(pieces, i):
            w, column = wgu[:, span_of(columns[i], width)], columns[i]
            x = jnp.concatenate(pieces, axis=0)
            wide = x.astype(f32)
            sq = jnp.sum(wide * wide, axis=1, keepdims=True)
            new = lax.dot_general(x * gn[column], w, (((1,), (1,)), ((), ())), preferred_element_type=f32)
            return new, jnp.broadcast_to(sq, (x.shape[0], 128))

        taken = 0
        for n, (k, parts) in enumerate(first):
            pieces = [r[...] for r in own[taken : taken + len(parts)]]
            taken += len(parts)
            new, sq = products(pieces, n)
            if n > 0:
                acc[...] += new
                acc_sq[...] += sq
            elif n_sums:
                acc[...] = held[0][...] + new
                acc_sq[...] = held[1][...] + sq
            else:
                acc[...] = new
                acc_sq[...] = sq

        rest = []
        for k, parts in second:
            rest.append((k, own[taken : taken + len(parts)]))
            taken += len(parts)
        for j in range(N):
            pieces = []
            for k, mine in rest:
                per = N // len(mine)
                pieces.append(mine[j // per][j % per * quarter : (j % per + 1) * quarter, :])
            new, sq = products(pieces, len(first) + j)
            for i, (k, _) in enumerate(rest):
                to, part = slice(k * quarter, (k + 1) * quarter), slice(i * quarter, (i + 1) * quarter)
                acc[to, :] += new[part]
                acc_sq[to, :] += sq[part]

        if last:
            scale = lax.rsqrt(acc_sq[:, :1] / (2 * N * width) + epsilon)

            def silu(gate, up):
                gate = gate * scale
                return (gate / (1.0 + jnp.exp(-gate)) * (up * scale)).astype(bf16)

            if main:
                inner[:, :main] = silu(acc[:, :main], acc[:, main : 2 * main])
            if main < hidden:
                inner[:, main:] = silu(acc[:, 2 * main : main + hidden], acc[:, main + hidden :])
            res = product(inner[...], down_block(wd, turned(at[1], 2), 0, width)).astype(bf16)
            p_a[...] = res[: rows // 2]
            p_b[...] = res[rows // 2 :]
            for j in range(N):
                w = down_block(wd, turned(at[1], j), 1, width)
                res = product(inner[2 * quarter : 3 * quarter, :], w).astype(bf16)
                (q_a, q_b)[j // 2][j % 2 * quarter : (j % 2 + 1) * quarter, :] = res

    wide, sq = shaped((rows, 2 * hidden), f32), shaped((rows, 128), f32)
    flops = 4 * hidden * width * rows * (len(first) + len(second))
    operands = [*(sums or ()), *chunks, gain, weights]
    if not last:
        return call(kernel, [wide, sq], at, [*operands, *after], "gate_up", 4 * flops)
    outs = [shaped((rows, hidden))] + [shaped((rows // 2, width))] * 4
    scratch = [pltpu.VMEM(wide.shape, f32), pltpu.VMEM(sq.shape, f32)]
    return call(kernel, outs, at, [*operands, w_down], "gate_up_down", 6 * flops, scratch)


def down(at, inner, w_down, ahead, halves):
    rows, hidden = inner.shape
    quarter = rows // N
    width = w_down.shape[1] // (2 * N)
    n = len(ahead)
    per = 2 if halves else 1

    def kernel(at, x, w, *outs):

        def put(which, start, res):
            size = rows // per
            for p in range(per):
                low, high = max(start, p * size), min(start + res.shape[0], (p + 1) * size)
                if low < high:
                    outs[which * per + p][low - p * size : high - p * size, :] = res[low - start : high - start]

        for i, r in enumerate(ahead):
            put(i, 0, product(x[...], down_block(w, turned(at[1], r), 0, width)).astype(bf16))
        starts = [(N - r) % N * quarter for r in ahead]
        xs = jnp.concatenate([x[s : s + quarter, :] for s in starts], axis=0)
        for j in range(N):
            res = product(xs, down_block(w, turned(at[1], j), 1, width)).astype(bf16)
            for i in range(n):
                put(n + i, j * quarter, res[i * quarter : (i + 1) * quarter])

    outs = [shaped((rows // per, width))] * (2 * n * per)
    return call(kernel, outs, at, [inner, w_down], "down", 12 * rows * hidden * width * n)


def below(at, parts):
    rows, width = parts[0].shape

    def kernel(at, *refs):
        for i in range(N):
            refs[N][i * rows : (i + 1) * rows, :] = refs[i][...]

    return call(kernel, shaped((N * rows, width)), at, parts, "below")


def halves(at, firsts, seconds):
    rows = firsts[0].shape[0] // 2
    operands = [v for pair in zip(firsts, seconds) for v in pair]

    def kernel(at, *refs):
        for i in range(len(operands)):
            start = i % 2 * rows
            refs[len(operands) + i][...] = refs[i][start : start + rows, :]

    return call(kernel, [shaped((rows, v.shape[1])) for v in operands], at, operands, "halves")


def add_halves(at, sets):
    rows, width = sets[0][0].shape
    half = rows // 2

    def kernel(at, *refs):
        outs = refs[4 * len(sets) :]
        for n in range(len(sets)):
            ahead, behind, a, b = refs[4 * n : 4 * n + 4]
            p, q = outs[2 * n : 2 * n + 2]
            p[:half, :] = wide_sum(ahead[:half, :], a[...]).astype(bf16)
            p[half:, :] = ahead[half:, :]
            q[:half, :] = behind[:half, :]
            q[half:, :] = wide_sum(behind[half:, :], b[...]).astype(bf16)

    outs = [shaped((rows, width))] * (2 * len(sets))
    return call(kernel, outs, at, [v for s in sets for v in s], "add_halves")


def sum_quarters(at, sets):
    rows, width = sets[0][0].shape
    quarter = rows // N

    def kernel(at, *refs):
        outs = refs[3 * len(sets) :]
        for n in range(len(sets)):
            for i in range(N):
                to = slice(i * quarter, (i + 1) * quarter)
                res = wide_sum(*[r[to, :] for r in refs[3 * n : 3 * n + 3]])
                outs[n * N + i][...] = res.astype(bf16)

    outs = [shaped((quarter, width))] * (N * len(sets))
    res = call(kernel, outs, at, [v for s in sets for v in s], "sum_quarters")
    return [res[n * N : (n + 1) * N] for n in range(len(sets))]


def sum_to_blocks(at, ones, twos):
    rows, width = ones[0].shape
    half, cols = rows // 2, width // 2

    def kernel(at, *refs):
        out = refs[2 * N]
        one = wide_sum(*[r[...] for r in refs[:N]]).astype(bf16)
        two = wide_sum(*[r[...] for r in refs[N : 2 * N]]).astype(bf16)
        for x in range(N):
            part = (one, two)[x // 2][:, x % 2 * cols : (x % 2 + 1) * cols]
            out[x * rows : (x + 1) * rows, :] = part

    return call(kernel, shaped((N * rows, cols)), at, [*ones, *twos], "sum_to_blocks")


def combine(at, outs, place, weights, hidden_one):
    rows, width = hidden_one.shape

    def kernel(at, o, where, w, h, first, second):
        slots = lax.broadcasted_iota(jnp.int32, (rows, o.shape[0]), 1)
        total = h[...].astype(f32)
        for j in range(TOP):
            taken = jnp.where(where[:, j : j + 1] == slots, 1.0, 0.0).astype(bf16)
            total = total + w[:, j : j + 1] * product(taken, o[...])
        total = total.astype(bf16)
        low, high = total[: rows // 2], total[rows // 2 :]
        even = (at[1] & 1) == 0
        first[...] = jnp.where(even, low, high)
        second[...] = jnp.where(even, high, low)

    return call(kernel, [shaped((rows // 2, width))] * 2, at, [outs, place, weights, hidden_one], "combine")


def experts_out(at, one, two, expert, gain):
    ones = [one] + [move_y(one, s) for s in (1, 2, 3)]
    twos = [two] + [move_z(two, s) for s in (1, 2, 3)]
    weights, done = keep_weights(expert[:2], one)
    w_down = expert[2]
    gain = gain.reshape(N, N, -1).swapaxes(0, 1).reshape(2 * N, 1, -1)
    ones, twos, done, gain = lax.optimization_barrier((ones, twos, done, gain))
    a0, b0 = below(at, ones), below(at, twos)
    a1, a3, b1, b3 = move_z(a0, 1), move_z(a0, -1), move_y(b0, 1), move_y(b0, -1)
    sums = gate_up(at, None, [(0, [a0])], [(0, [b0])], weights, gain, after=[done])
    sums, a1, a3, b1, b3 = lax.optimization_barrier((sums, a1, a3, b1, b3))
    a1_low, a3_high, b1_low, b3_high = halves(at, [a1, b1], [a3, b3])
    a2 = [move_z(a1_low, 1), move_z(a3_high, -1)]
    b2 = [move_y(b1_low, 1), move_y(b3_high, -1)]
    sums = gate_up(at, sums, [(1, [a1]), (3, [a3])], [(1, [b1]), (3, [b3])], weights, gain)
    inner, p2a, p2b, q2a, q2b = gate_up(at, sums, [(2, a2)], [(2, b2)], weights, gain, w_down)
    p2a, p2b = move_z(p2a, 1), move_z(p2b, -1)
    q2a, q2b = move_y(q2a, 1), move_y(q2b, -1)
    p1, p3, q1, q3 = down(at, inner, w_down, [1, 3], False)
    p1, p3, q1, q3 = add_halves(at, [(p1, p3, p2a, p2b), (q1, q3, q2a, q2b)])
    p1, p3 = move_z(p1, 1), move_z(p3, -1)
    q1, q3 = move_y(q1, 1), move_y(q3, -1)
    p0, q0 = down(at, inner, w_down, [0], False)
    p, q = sum_quarters(at, [(p0, p1, p3), (q0, q1, q3)])
    p = [p[0]] + [move_y(p[N - r], r) for r in (1, 2, 3)]
    q = [q[0]] + [move_z(q[r], r) for r in (1, 2, 3)]
    return sum_to_blocks(at, p, q)


def per_device(
    queries,
    keys,
    values,
    prefix_state,
    out_gain,
    out_weight,
    resid,
    ffn_gain,
    expert_ids,
    route_weights,
    gate_weight,
    up_weight,
    down_weight,
):
    ctx, mdl = lax.axis_index("ctx"), lax.axis_index("mdl")
    y, z = ctx // N, ctx % N
    x, c = mdl // 2, mdl % 2
    rows = queries.shape[0]
    cols = resid.shape[1]
    experts = 2 * N
    cap = 3 * rows * TOP // (2 * experts)

    chosen = expert_ids[:, :, None] == jnp.arange(experts, dtype=jnp.int32)
    uses = jnp.sum(chosen.astype(jnp.int32), axis=1)
    slots = jnp.cumsum(uses, axis=0) - uses
    slot_of = jnp.sum(jnp.where(chosen, slots[:, None, :], 0), axis=2)
    high = lax.reduce_precision(route_weights, 8, 7)
    middle = lax.reduce_precision(route_weights - high, 8, 7)
    low = route_weights - high - middle
    routing = jnp.concatenate([expert_ids.astype(f32), slot_of.astype(f32), high, middle, low], axis=1)
    routing = jnp.pad(routing.astype(bf16), ((0, 0), (0, 128 - 5 * TOP)))
    half = cols // 2
    own = by_parity(z, resid[:, :half], resid[:, half:])
    own = [jnp.concatenate([part, routing], axis=1) for part in own]
    groups_y = [[a * N + b for a in range(N)] for b in range(N)]
    w_full = lax.all_gather(out_weight, "ctx", axis=1, tiled=True, axis_index_groups=groups_y)
    at = jnp.stack([y, z, x, c]).astype(jnp.int32)
    carried = carried_states(spans(at, keys, values), prefix_state, y, z)
    attn = attend(at, queries, values, scores_of(at, queries, keys), carried, out_gain)

    blocks = [attn] + [move_z(attn, s) for s in (1, 2, 3)]
    blocks[1], own = lax.optimization_barrier((blocks[1], own))
    own = by_parity(z, trade(own[0], 0), trade(own[1], 1))
    own = jnp.concatenate(own, axis=0)
    own_resid, routing = own[:, :half], own[:, half : half + 5 * TOP].astype(f32)
    routing = [routing[:, i * TOP : (i + 1) * TOP] for i in range(5)]
    block = jnp.repeat(jnp.arange(2, dtype=jnp.int32), rows)[:, None] * cap
    place = (routing[0] * (2 * cap) + routing[1]).astype(jnp.int32) + block
    weights = routing[2] + routing[3] + routing[4]
    placing = jnp.any(place[:, :, None] == jnp.arange(2 * experts * cap, dtype=jnp.int32), axis=1).astype(bf16).T
    given, kept = project(at, blocks, w_full)
    given = move_m(given, 0, 1)
    parts = pair_sums(at, kept, given)
    parts = [parts[0]] + [move_m(parts[s], s, 0) for s in (1, 2, 3)]
    hidden_one, picked = hidden_and_picked(at, parts, own_resid, placing)
    picked = lax.all_to_all(picked, "mdl", 0, 0, tiled=True).reshape(2, 2, 2, 2 * cap, half)
    one, two = [picked[h].transpose(1, 2, 0, 3).reshape(N * cap, cols) for h in range(2)]
    expert = [jnp.swapaxes(gate_weight[0], 0, 1), jnp.swapaxes(up_weight[0], 0, 1), down_weight[0]]
    outs = experts_out(at, one, two, expert, ffn_gain)
    outs = lax.all_to_all(outs, "mdl", 0, 0, tiled=True)
    first, second = combine(at, outs, place, weights, hidden_one)
    return jnp.concatenate(by_parity(z, trade(first, 0), trade(second, 1)), axis=1)


def solution(mesh):
    placed = (
        P("ctx", "mdl"),
        P("ctx", "mdl"),
        P("ctx", "mdl"),
        P("mdl", None, None),
        P("mdl"),
        P("mdl", "ctx"),
        P("ctx", "mdl"),
        P(),
        P("ctx", None),
        P("ctx", None),
        P("mdl", None, "ctx"),
        P("mdl", None, "ctx"),
        P("mdl", "ctx", None),
    )
    return jax.shard_map(
        per_device, mesh=mesh, in_specs=placed, out_specs=P("ctx", "mdl"), check_vma=False
    )
```
